256 devices in a mesh: users: 64 (over z, x, core), seq: 4 (over y).
Axes of the slice: x: 4, y: 4, z: 8, core: 2. Of those that a mesh axis runs over, the one named last changes fastest.
Arguments:
- tokens: bfloat16 [65536, 1024], P(('users', 'seq')), may hold values from -24 to 24, as said below
- item_table: bfloat16 [16384, 1024], P('users'), may hold values from -24 to 24, as said below
- w_in: bfloat16 [1024, 4096], replicated, may hold values from -0.1875 to 0.1875
- w_out: bfloat16 [1024, 1024], replicated, may hold values from -0.1875 to 0.1875
- gain_in: float32 [1024], replicated, may hold values from 0.25 to 1.75
- gain_attn: float32 [1024], replicated, may hold values from 0.25 to 1.75
- hist_len: int32 [128], P('users'), may hold values from 1 to 896, as said below
- row_start: int32 [128], P('users'), may hold values from 0 to 65408, as said below
- impressions: int32 [128, 1024], P('users', 'seq'), may hold values from 0 to 16383, as said below
- item_slot: int32 [16384], replicated, may hold values from 0 to 16383, as said below
Outputs:
- hist_out: bfloat16 [65536, 1024], P(('users', 'seq'))
- cand_out: bfloat16 [128, 1024, 1024], P('users', 'seq')
The draws below stay inside these ranges and needn't reach their ends.
Inputs may be any that keep to these rules, and one draw needn't show every extreme that they name: `hist_len`: users 2g and 2g+1 are the histories of users index g; each history of length n fills ceil(n / 128) blocks, and the two together fill all 1024 rows of their users index. row_start[2g] = g * 1024; row_start[2g+1] = row_start[2g] + 128 * ceil(hist_len[2g] / 128). A permutation: item i is row item_slot[i] of item_table, held by users index item_slot[i] // 256. Of the 512 impressions on one device (the users of one users index, the candidates of one seq index), at most 16 are items held by any one users index. Ids may repeat. `tokens`: entries are of order one, with rows and columns of different scales. `item_table`: entries are of order one, with rows and columns of different scales.
All inputs are finite; a program needn't handle non-finite values.
Results may differ from the reference program's by a relative error of at most 0.008.
Values may be sent and summed in bfloat16 or wider, within the bound.
A program may use at most 128 MiB of HBM per device.

```python
import math
import jax
import jax.numpy as jnp
from jax import lax

D = 1024
HEADS = 8
BLOCK = 128
USERS_GRP = 2
CAND_DEV = 256
ITEMS_DEV = 256
GROUP_ROWS = 1024
TOKENS = 65536
USERS = 128
CAND = 1024
ITEMS = 16384
CAP = 16


def scale_rows(key, noise):
    first_key, second_key = jax.random.split(key, 2)
    row_scale = jnp.exp(jax.random.uniform(first_key, (noise.shape[0], 1), jnp.float32, math.log(0.3), math.log(3.0)))
    column_scale = jnp.exp(jax.random.uniform(second_key, (1, noise.shape[1]), jnp.float32, math.log(0.5), math.log(2.0)))
    return noise * row_scale * column_scale


def draw_tokens(key, part):
    key = jax.random.fold_in(key, 11)
    first_key, second_key = jax.random.split(key, 2)
    noise = jnp.clip(jax.random.normal(first_key, (TOKENS, D), jnp.float32), -4.0, 4.0)
    return scale_rows(second_key, noise).astype(jnp.bfloat16)


def draw_item_table(key, part):
    key = jax.random.fold_in(key, 23)
    first_key, second_key = jax.random.split(key, 2)
    noise = jnp.clip(jax.random.normal(first_key, (ITEMS, D), jnp.float32), -4.0, 4.0)
    return scale_rows(second_key, noise).astype(jnp.bfloat16)


def layout(key):
    group_count = USERS // USERS_GRP
    block_count = GROUP_ROWS // BLOCK
    key_one, key_two, key_three, key_four = jax.random.split(key, 4)
    first_blocks = jax.random.randint(key_one, (group_count,), 1, block_count)
    forced = jax.random.randint(key_four, (), 0, group_count)
    group_ids = jnp.arange(group_count)
    is_forced = (group_ids == forced) | (group_ids == group_count - 1)
    first_blocks = jnp.where(is_forced, block_count - 1, first_blocks)
    second_blocks = block_count - first_blocks
    first_len = jax.random.randint(key_two, (group_count,), BLOCK * (first_blocks - 1) + 1, BLOCK * first_blocks + 1)
    second_len = jax.random.randint(key_three, (group_count,), BLOCK * (second_blocks - 1) + 1, BLOCK * second_blocks + 1)
    first_len = jnp.where(is_forced, BLOCK * (block_count - 1), first_len)
    second_len = jnp.where(is_forced, 1, second_len)
    row_base = group_ids * GROUP_ROWS
    lengths = jnp.stack([first_len, second_len], axis=1).reshape(-1)
    starts = jnp.stack([row_base, row_base + BLOCK * first_blocks], axis=1).reshape(-1)
    return (lengths.astype(jnp.int32), starts.astype(jnp.int32))


def draw_hist_len(key, part):
    lengths, starts = layout(key)
    return lengths


def draw_row_start(key, part):
    lengths, starts = layout(key)
    return starts


def catalog(key):
    key_one, key_two, key_three = jax.random.split(key, 3)
    slots = jax.random.permutation(key_one, ITEMS).astype(jnp.int32)
    inverse = jnp.argsort(slots).astype(jnp.int32)
    owner_count = ITEMS // ITEMS_DEV
    seq_count = CAND // CAND_DEV
    wanted = USERS_GRP * CAND_DEV
    hottest = jax.random.randint(key_two, (), 0, owner_count)

    def one_device(device_key):
        pick_key, local_key, order_key = jax.random.split(device_key, 3)
        picks = jax.random.permutation(pick_key, (owner_count - 1) * CAP)[:wanted - CAP]
        others = picks // CAP
        owner_ids = others + (others >= hottest).astype(others.dtype)
        owner_ids = jnp.concatenate([jnp.full((CAP,), hottest, owner_ids.dtype), owner_ids])
        local_rows = jax.random.randint(local_key, (wanted,), 0, ITEMS_DEV)
        chosen = inverse[owner_ids * ITEMS_DEV + local_rows]
        return chosen[jax.random.permutation(order_key, wanted)]
    device_keys = jax.random.split(key_three, owner_count * seq_count)
    ids_all = jax.vmap(one_device)(device_keys)
    ids_all = ids_all.reshape(owner_count, seq_count, USERS_GRP, CAND_DEV).transpose(0, 2, 1, 3)
    return (slots, ids_all.reshape(USERS, CAND).astype(jnp.int32))


def draw_item_slot(key, part):
    slots, chosen = catalog(key)
    return slots


def draw_impressions(key, part):
    slots, chosen = catalog(key)
    return chosen


def bell_draw(stream_key, extent, deviation, limit, kind=jnp.bfloat16):
    drawn = deviation * jax.random.normal(stream_key, extent, jnp.float32)
    return jnp.clip(drawn, min=-limit, max=limit).astype(kind)


def setup_inputs(seed: int = 0) -> dict:
    arg_keys = jax.random.split(jax.random.key(seed), 11)
    return {
        "tokens": draw_tokens(jax.random.fold_in(arg_keys[10], 71), 0),
        "item_table": draw_item_table(jax.random.fold_in(arg_keys[10], 71), 0),
        "w_in": bell_draw(arg_keys[2], (D, 4 * D), D ** -0.5, 0.1875),
        "w_out": bell_draw(arg_keys[3], (D, D), D ** -0.5, 0.1875),
        "gain_in": jnp.clip(1.0 + 0.15 * jax.random.normal(arg_keys[4], (D,), jnp.float32), 0.25, 1.75),
        "gain_attn": jnp.clip(1.0 + 0.15 * jax.random.normal(arg_keys[5], (D,), jnp.float32), 0.25, 1.75),
        "hist_len": draw_hist_len(jax.random.fold_in(arg_keys[10], 71), 0),
        "row_start": draw_row_start(jax.random.fold_in(arg_keys[10], 71), 0),
        "impressions": draw_impressions(jax.random.fold_in(arg_keys[10], 71), 0),
        "item_slot": draw_item_slot(jax.random.fold_in(arg_keys[10], 71), 0),
    }


epsilon = 1e-05

def layer_norm(values, gain_vec):
    centered = values - lax.optimization_barrier(jnp.mean(values, axis=-1, keepdims=True))
    spread = lax.optimization_barrier(jnp.mean(centered * centered, axis=-1, keepdims=True))
    return centered * lax.rsqrt(spread + epsilon) * gain_vec.astype(jnp.float32)

def project(rows_in, w_in, gain_in):
    model_width = rows_in.shape[1]
    normed = layer_norm(rows_in.astype(jnp.float32), gain_in).astype(jnp.bfloat16)
    projected = jnp.dot(normed, w_in, preferred_element_type=jnp.float32)
    gate_part = jax.nn.silu(projected[:, :model_width]).astype(jnp.bfloat16)
    value_part = projected[:, model_width:2 * model_width].astype(jnp.bfloat16)
    query_part = projected[:, 2 * model_width:3 * model_width].astype(jnp.bfloat16)
    key_part = projected[:, 3 * model_width:].astype(jnp.bfloat16)
    return (gate_part, value_part, query_part, key_part)

def attend_all(queries, keys_in, values_in, allowed):
    query_count = queries.shape[0]
    key_count = keys_in.shape[0]
    model_width = queries.shape[1]
    head_dim = model_width // HEADS
    scores = jnp.einsum('qhd,khd->hqk', queries.reshape(query_count, HEADS, head_dim).astype(jnp.float32), keys_in.reshape(key_count, HEADS, head_dim).astype(jnp.float32)) * (1.0 / math.sqrt(head_dim))
    weights = jnp.where(allowed[None], jax.nn.silu(scores), 0.0).astype(jnp.bfloat16)
    attended = jnp.einsum('hqk,khd->qhd', weights.astype(jnp.float32), values_in.reshape(key_count, HEADS, head_dim).astype(jnp.float32))
    return attended.reshape(query_count, model_width)

def finish(rows_in, attended, gate_part, gain_attn, w_out):
    mixed_rows = (layer_norm(attended, gain_attn) * gate_part.astype(jnp.float32)).astype(jnp.bfloat16)
    summed = rows_in.astype(jnp.float32) + jnp.dot(mixed_rows, w_out, preferred_element_type=jnp.float32)
    return summed.astype(jnp.bfloat16)

def reference(tokens, item_table, w_in, w_out, gain_in, gain_attn, hist_len, row_start, impressions, item_slot):
    model_width = tokens.shape[1]
    group_count = USERS // USERS_GRP

    def one_group(group_index):
        row_base = (group_index * GROUP_ROWS).astype(jnp.int32)
        group_rows = lax.dynamic_slice_in_dim(tokens, row_base, GROUP_ROWS, 0)
        user_base = (group_index * USERS_GRP).astype(jnp.int32)
        group_len = lax.dynamic_slice_in_dim(hist_len, user_base, USERS_GRP, 0)
        group_start = lax.dynamic_slice_in_dim(row_start, user_base, USERS_GRP, 0) - row_base
        position = jnp.arange(GROUP_ROWS, dtype=jnp.int32)
        row_user = (position >= group_start[1]).astype(jnp.int32)
        row_end = jnp.where(row_user == 1, group_start[1] + group_len[1], group_start[0] + group_len[0])
        row_live = position < row_end
        gate_part, value_part, query_part, key_part = project(group_rows, w_in, gain_in)
        causal = (row_user[:, None] == row_user[None, :]) & row_live[:, None] & row_live[None, :] & (position[None, :] <= position[:, None])
        hist_rows = finish(group_rows, attend_all(query_part, key_part, value_part, causal), gate_part, gain_attn, w_out)
        picked = lax.dynamic_slice_in_dim(impressions, user_base, USERS_GRP, 0).reshape(-1)
        embedded = item_table[item_slot[picked]]
        cand_parts = project(embedded, w_in, gain_in)
        cand_user = jnp.arange(USERS_GRP * CAND, dtype=jnp.int32) // CAND
        visible = (cand_user[:, None] == row_user[None, :]) & row_live[None, :]
        cand_rows = finish(embedded, attend_all(cand_parts[2], key_part, value_part, visible), cand_parts[0], gain_attn, w_out)
        return (hist_rows, cand_rows.reshape(USERS_GRP, CAND, model_width))
    hist_all, cand_all = lax.map(one_group, jnp.arange(group_count, dtype=jnp.int32))
    return (hist_all.reshape(TOKENS, model_width), cand_all.reshape(USERS, CAND, model_width))
```

```python
import functools
import math

import jax
import jax.numpy as jnp
from jax import lax
from jax.experimental import pallas as pl
from jax.experimental.pallas import tpu as pltpu
from jax.sharding import PartitionSpec as P

MESH = pl.DeviceIdType.MESH
HEADS = 8
WIDTH = 1024
HEAD_DIM = WIDTH // HEADS
ROWS = 256
CANDS = 512
KEYS = 1024
CAP = 16
OWNERS = 64
CHUNK = 128
epsilon = 1e-05
F32 = jnp.float32
BF16 = jnp.bfloat16
I32 = jnp.int32


def group_dz(q):
    return [0, 1, 7, 2, 6, 3, 5, 4][q]


def group_of_dz(dz):
    return jnp.where(dz == 0, 0, jnp.where(dz <= 4, 2 * dz - 1, 2 * (8 - dz)))


def layer_norm(values, gain_row):
    centered = values - jnp.mean(values, axis=-1, keepdims=True)
    spread = jnp.mean(centered * centered, axis=-1, keepdims=True)
    return centered * lax.rsqrt(spread + epsilon) * gain_row


def half_silu(half):
    return half + half * jnp.tanh(half)


def dot(a, b):
    return jnp.dot(a, b, preferred_element_type=F32)


def dot_nt(a, b):
    return lax.dot_general(a, b, (((1,), (1,)), ((), ())), preferred_element_type=F32)


def dot_tn(a, b):
    return lax.dot_general(a, b, (((0,), (0,)), ((), ())), preferred_element_type=F32)


def iota(shape, dim):
    return lax.broadcasted_iota(I32, shape, dim)


def kernel(
    hist_len, row_start, tokens, table, w_in, w_out, gain_in, gain_attn, wanted, item_slot,
    hist_out, cand_out,
    win, wout, normed, keys, values, hgate, hquery, attended, scale_mask,
    requests, asked, served, embedded, cgate, cquery, csorted, place,
    w_sem, req_send, req_recv, row_send, row_recv, ring_send, ring_recv,
):
    me = lax.axis_index("users")
    y = lax.axis_index("seq")
    z, x, c = me // 8, (me // 2) % 4, me % 2
    half_scale = 0.5 / math.sqrt(HEAD_DIM)

    def device(zz, xx, cc, yy):
        return {"users": ((zz + 8) % 8) * 8 + ((xx + 4) % 4) * 2 + (cc + 2) % 2, "seq": (yy + 4) % 4}

    def remote(src, dst, send, recv, target):
        return pltpu.make_async_remote_copy(
            src_ref=src, dst_ref=dst, send_sem=send, recv_sem=recv, device_id=target, device_id_type=MESH
        )

    weight_copies = [
        pltpu.make_async_copy(w_in.at[:, pl.ds(b * WIDTH, WIDTH)], win.at[b], w_sem.at[b]) for b in range(4)
    ]
    weight_copies.append(pltpu.make_async_copy(w_out, wout, w_sem.at[4]))
    for copy in weight_copies:
        copy.start()

    barrier = pltpu.get_barrier_semaphore()
    for q in range(8):
        for k in range(8):
            if q or k:
                pl.semaphore_signal(
                    barrier, inc=1, device_id=device(z + group_dz(q), x + k // 2, c + k % 2, y), device_id_type=MESH
                )
    for dy in (1, 3):
        pl.semaphore_signal(barrier, inc=1, device_id=device(z, x, c, y + dy), device_id_type=MESH)

    ids = jnp.concatenate([wanted[0:1, :], wanted[1:2, :]], axis=1)
    pick_high = (iota((128, CANDS), 0) == (ids >> 7)).astype(BF16)
    slots_2d = item_slot[...]
    at_high = dot_tn((slots_2d >> 7).astype(F32).astype(BF16), pick_high) * 128.0 + dot_tn(
        (slots_2d & 127).astype(F32).astype(BF16), pick_high
    )
    slot = jnp.sum(jnp.where(iota((128, CANDS), 0) == (ids & 127), at_high, 0.0), axis=0, keepdims=True)
    slot = slot.astype(I32)
    owner, local = slot >> 8, slot & 255
    dz = ((owner >> 3) - z) & 7
    dx = (((owner >> 1) & 3) - x) & 3
    dc = (owner - c) & 1
    lot = group_of_dz(dz) * 8 + dx * 2 + dc
    is_lot = iota((OWNERS, CANDS), 0) == lot
    lot_hot = is_lot.astype(BF16)
    earlier = (iota((CANDS, CANDS), 0) < iota((CANDS, CANDS), 1)).astype(BF16)
    before = dot(lot_hot, earlier)
    total = jnp.sum(is_lot.astype(F32), axis=1, keepdims=True)
    rank = jnp.sum(jnp.where(is_lot, before, 0.0), axis=0, keepdims=True).astype(I32)
    base = jnp.sum(jnp.where(iota((OWNERS, CANDS), 0) < lot, total, 0.0), axis=0, keepdims=True)
    position = base.astype(I32) + rank
    lane = (lot & 7) * CAP + rank
    lane_local = jnp.where(iota((128, CANDS), 0) == lane, local, 0).astype(F32).astype(BF16)
    request_rows = dot_nt(lot_hot, lane_local).astype(I32)
    for j in range(OWNERS):
        requests[j] = request_rows[j : j + 1, :]
    asked[0] = request_rows[0:1, :]

    normed[y] = layer_norm(tokens[...].astype(F32), gain_in[...]).astype(BF16)

    pl.semaphore_wait(barrier, 65)

    for q in range(8):
        for k in range(8):
            if q or k:
                j = q * 8 + k
                remote(
                    requests.at[j], asked.at[j], req_send, req_recv.at[q],
                    device(z + group_dz(q), x + k // 2, c + k % 2, y),
                ).start()
    up, down = device(z, x, c, y + 1), device(z, x, c, y - 1)
    own, below, above = normed.at[y], normed.at[(y + 3) % 4], normed.at[(y + 1) % 4]
    remote(own, own, ring_send.at[0], ring_recv.at[0], up).start()
    remote(own, own, ring_send.at[1], ring_recv.at[1], down).start()

    slot_user = lot * CAP + rank + jnp.where(iota((1, CANDS), 1) >= CANDS // 2, 1024, 0)
    sorted_slot = jnp.sum(
        jnp.where(iota((CANDS, CANDS), 0) == position, slot_user, 0).astype(F32), axis=1, keepdims=True
    ).astype(I32)
    position_column = jnp.sum(
        jnp.where(iota((CANDS, CANDS), 0) == iota((CANDS, CANDS), 1), position, 0).astype(F32),
        axis=1,
        keepdims=True,
    ).astype(I32)
    place[:, 0:1] = sorted_slot
    place[:, 1:2] = position_column

    for q in range(8):
        first = 1 if q == 0 else 0
        lots = pl.ds(q * 8 + first, 8 - first)
        remote(asked.at[lots], asked.at[lots], req_send, req_recv.at[q], up).wait_recv()
        gathered = asked[q * 8]
        for k in range(1, 8):
            gathered = gathered + asked[q * 8 + k]
        pick = (iota((ROWS, CHUNK), 0) == gathered).astype(BF16)
        served[pl.ds(q * CHUNK, CHUNK), :] = dot_tn(pick, table[...]).astype(BF16)
        for k in range(first, 8):
            rows = pl.ds(q * CHUNK + k * CAP, CAP)
            remote(
                served.at[rows], embedded.at[rows], row_send, row_recv.at[q],
                device(z - group_dz(q), x - k // 2, c - k % 2, y),
            ).start()
    embedded[pl.ds(0, CAP), :] = served[pl.ds(0, CAP), :]

    def project(rows_value, block, write):
        def step(n, carry):
            columns = pl.ds(pl.multiple_of(n * 256, 256), 256)
            write(columns, dot(rows_value(), win[block, :, columns]))
            return carry

        lax.fori_loop(0, WIDTH // 256, step, 0)

    def project_keys(block):
        rows = pl.ds(pl.multiple_of(block * ROWS, ROWS), ROWS)

        def write_value(columns, out):
            values[rows, columns] = out.astype(BF16)

        def write_key(columns, out):
            keys[rows, columns] = out.astype(BF16)

        project(lambda: normed[block], 1, write_value)
        project(lambda: normed[block], 3, write_key)

    def write_hgate(columns, out):
        hgate[:, columns] = half_silu(out * 0.5).astype(BF16)

    def write_hquery(columns, out):
        hquery[:, columns] = out.astype(BF16)

    for copy in weight_copies:
        copy.wait()
    project(lambda: normed[y], 0, write_hgate)
    project(lambda: normed[y], 2, write_hquery)
    project_keys(y)

    upper, lower = pl.ds(0, ROWS // 2), pl.ds(ROWS // 2, ROWS // 2)
    remote(below, below, ring_send.at[0], ring_recv.at[0], up).wait()
    remote(below.at[upper], below.at[upper], ring_send.at[0], ring_recv.at[2], up).start()
    remote(above, above, ring_send.at[1], ring_recv.at[1], down).wait()
    remote(above.at[lower], above.at[lower], ring_send.at[1], ring_recv.at[3], down).start()
    project_keys((y + 3) % 4)
    project_keys((y + 1) % 4)
    far = normed.at[(y + 2) % 4]
    remote(below.at[upper], far.at[upper], ring_send.at[0], ring_recv.at[2], up).wait()
    remote(above.at[lower], far.at[lower], ring_send.at[1], ring_recv.at[3], down).wait()
    project_keys((y + 2) % 4)

    group_base = me * KEYS
    second = row_start[1] - group_base
    end_first, end_second = row_start[0] - group_base + hist_len[0], second + hist_len[1]

    def locate(spot):
        user = (spot >= second).astype(I32)
        return user, spot < jnp.where(user == 1, end_second, end_first)

    key_spot = iota((1, KEYS), 1)
    key_user, key_live = locate(key_spot)
    query_spot = y * ROWS + iota((ROWS, 1), 0)
    query_user, query_live = locate(query_spot)

    def attend(rows, query):
        def head(h, carry):
            columns = pl.ds(pl.multiple_of(h * HEAD_DIM, HEAD_DIM), HEAD_DIM)
            scores = dot_nt(query[:, columns], keys[:, columns])
            weights = half_silu(scores * scale_mask[0:rows, :]).astype(BF16)
            attended[0:rows, columns] = dot(weights, values[:, columns])
            return carry

        lax.fori_loop(0, HEADS, head, 0)

    def finish(rows, residual, gate, write):
        mixed = (layer_norm(attended[0:rows, :], gain_attn[...]) * gate[...].astype(F32)).astype(BF16)
        for n in range(WIDTH // 256):
            columns = pl.ds(n * 256, 256)
            write(columns, (residual(columns) + dot(mixed, wout[:, columns])).astype(BF16))

    allowed = (
        (query_user == key_user)
        & (query_live & key_live)
        & (key_spot <= query_spot)
    )
    scale_mask[...] = jnp.where(allowed, half_scale, 0.0)
    attend(ROWS, hquery)

    def write_hist(columns, out):
        hist_out[:, columns] = out

    finish(ROWS, lambda columns: tokens[:, columns].astype(F32), hgate, write_hist)

    def wait_group(q):
        rows = pl.ds(CAP, CHUNK - CAP) if q == 0 else pl.ds(q * CHUNK, CHUNK)
        remote(embedded.at[rows], embedded.at[rows], row_send, row_recv.at[q], up).wait_recv()

    for q in range(4):
        wait_group(q)
    for piece in range(4):
        wait_group(piece + 4)
        slot_column = place[pl.ds(piece * CHUNK, CHUNK), 0:1]
        pick = (iota((CHUNK, 5 * CHUNK), 1) + piece * CHUNK == (slot_column & 1023)).astype(BF16)
        rows_in = dot(pick, embedded[pl.ds(piece * CHUNK, 5 * CHUNK), :])
        cand_normed = layer_norm(rows_in, gain_in[...]).astype(BF16)
        for n in range(WIDTH // 256):
            columns = pl.ds(n * 256, 256)
            cgate[:, columns] = half_silu(dot(cand_normed, win[0, :, columns]) * 0.5).astype(BF16)
            cquery[:, columns] = dot(cand_normed, win[2, :, columns]).astype(BF16)
        visible = ((slot_column >> 10) == key_user) & key_live
        scale_mask[0:CHUNK, :] = jnp.where(visible, half_scale, 0.0)
        attend(CHUNK, cquery)

        def write_sorted(columns, out, piece=piece):
            csorted[pl.ds(piece * CHUNK, CHUNK), columns] = out

        finish(CHUNK, lambda columns, rows_in=rows_in: rows_in[:, columns.start : columns.start + 256], cgate, write_sorted)

    for half in range(2):
        spots = place[pl.ds(half * 256, 256), 1:2]
        unpick = (iota((256, CANDS), 1) == spots).astype(BF16)
        cand_out[half] = dot(unpick, csorted[...]).astype(BF16)

    lots = pl.ds(1, OWNERS - 1)
    remote(requests.at[lots], requests.at[lots], req_send, req_recv.at[0], up).wait_send()
    rows = pl.ds(CAP, 1024 - CAP)
    remote(served.at[rows], served.at[rows], row_send, row_recv.at[0], up).wait_send()


def body(
    tokens, item_table, w_in, w_out, gain_in, gain_attn, hist_len, row_start, impressions, item_slot
):
    vmem = pl.BlockSpec(memory_space=pltpu.VMEM)
    smem = pl.BlockSpec(memory_space=pltpu.SMEM)
    anywhere = pl.BlockSpec(memory_space=pl.ANY)
    return pl.pallas_call(
        kernel,
        out_shape=(
            jax.ShapeDtypeStruct((ROWS, WIDTH), BF16),
            jax.ShapeDtypeStruct((2, CANDS // 2, WIDTH), BF16),
        ),
        in_specs=[smem, smem, vmem, vmem, anywhere, anywhere, vmem, vmem, vmem, vmem],
        out_specs=(vmem, vmem),
        scratch_shapes=[
            pltpu.VMEM((4, WIDTH, WIDTH), BF16),
            pltpu.VMEM((WIDTH, WIDTH), BF16),
            pltpu.VMEM((4, ROWS, WIDTH), BF16),
            pltpu.VMEM((KEYS, WIDTH), BF16),
            pltpu.VMEM((KEYS, WIDTH), BF16),
            pltpu.VMEM((ROWS, WIDTH), BF16),
            pltpu.VMEM((ROWS, WIDTH), BF16),
            pltpu.VMEM((ROWS, WIDTH), F32),
            pltpu.VMEM((ROWS, KEYS), F32),
            pltpu.VMEM((OWNERS, 1, 128), I32),
            pltpu.VMEM((OWNERS, 1, 128), I32),
            pltpu.VMEM((OWNERS * CAP, WIDTH), BF16),
            pltpu.VMEM((OWNERS * CAP, WIDTH), BF16),
            pltpu.VMEM((CHUNK, WIDTH), BF16),
            pltpu.VMEM((CHUNK, WIDTH), BF16),
            pltpu.VMEM((CANDS, WIDTH), BF16),
            pltpu.VMEM((CANDS, 128), I32),
            pltpu.SemaphoreType.DMA((5,)),
            pltpu.SemaphoreType.DMA,
            pltpu.SemaphoreType.DMA((8,)),
            pltpu.SemaphoreType.DMA,
            pltpu.SemaphoreType.DMA((8,)),
            pltpu.SemaphoreType.DMA((2,)),
            pltpu.SemaphoreType.DMA((4,)),
        ],
        compiler_params=pltpu.CompilerParams(
            collective_id=0, has_side_effects=True, vmem_limit_bytes=56 * 2**20
        ),
    )(
        hist_len, row_start, tokens, item_table, w_in, w_out,
        gain_in.reshape(1, WIDTH), gain_attn.reshape(1, WIDTH),
        impressions, item_slot.reshape(128, 128),
    )


def solution(mesh):
    placed = (
        P(("users", "seq"), None),
        P("users", None),
        P(),
        P(),
        P(),
        P(),
        P("users"),
        P("users"),
        P("users", "seq"),
        P(),
    )
    return jax.shard_map(
        body,
        mesh=mesh,
        in_specs=placed,
        out_specs=(P(("users", "seq"), None), P("users", "seq", None)),
        check_vma=False,
    )
```

```python
import functools
import math

import jax
import jax.numpy as jnp
from jax import lax
from jax.experimental import pallas as pl
from jax.experimental.pallas import tpu as pltpu
from jax.sharding import PartitionSpec as P

MESH = pl.DeviceIdType.MESH
HEADS = 8
WIDTH = 1024
HEAD_DIM = WIDTH // HEADS
ROWS = 256
CANDS = 512
KEYS = 1024
CAP = 16
OWNERS = 64
NEAR = 5
CHUNK = 128
epsilon = 1e-05
F32 = jnp.float32
BF16 = jnp.bfloat16
I32 = jnp.int32


def group_dz(q):
    return [0, 1, 7, 2, 6, 3, 5, 4][q]


def group_of_dz(dz):
    return jnp.where(dz == 0, 0, jnp.where(dz <= 4, 2 * dz - 1, 2 * (8 - dz)))


def layer_norm(values, gain_row):
    centered = values - jnp.mean(values, axis=-1, keepdims=True)
    spread = jnp.mean(centered * centered, axis=-1, keepdims=True)
    return centered * lax.rsqrt(spread + epsilon) * gain_row


def half_silu(half):
    return half + half * jnp.tanh(half)


def dot(a, b):
    return jnp.dot(a, b, preferred_element_type=F32)


def dot_nt(a, b):
    return lax.dot_general(a, b, (((1,), (1,)), ((), ())), preferred_element_type=F32)


def dot_tn(a, b):
    return lax.dot_general(a, b, (((0,), (0,)), ((), ())), preferred_element_type=F32)


def iota(shape, dim):
    return lax.broadcasted_iota(I32, shape, dim)


def kernel(
    hist_len, row_start, tokens, table, w_in, w_out, gain_in, gain_attn, wanted, item_slot,
    hist_done, keys_done, values_done, rows_done, gate_done, query_done,
    win, wout, normed, keys, values, hgate, hquery, attended, scale_mask, hist,
    requests, asked, asked_far, far_table, served, served_far, embedded,
    rows_in, rows_out, cnormed, cgate, cquery, place,
    w_sem, req_send, req_recv, far_req_recv, row_send, far_row_send, row_recv,
    ring_send, ring_recv, copy_up, copy_down, copy_recv, out_sem,
):
    me = lax.axis_index("users")
    y = lax.axis_index("seq")
    z, x, c = me // 8, (me // 2) % 4, me % 2
    half_scale = 0.5 / math.sqrt(HEAD_DIM)

    def device(zz, xx, cc, yy):
        return {"users": ((zz + 8) % 8) * 8 + ((xx + 4) % 4) * 2 + (cc + 2) % 2, "seq": (yy + 4) % 4}

    def remote(src, dst, send, recv, target):
        return pltpu.make_async_remote_copy(
            src_ref=src, dst_ref=dst, send_sem=send, recv_sem=recv, device_id=target, device_id_type=MESH
        )

    weight_copies = [
        pltpu.make_async_copy(w_in.at[:, pl.ds(b * WIDTH, WIDTH)], win.at[b], w_sem.at[b]) for b in range(4)
    ]
    weight_copies.append(pltpu.make_async_copy(w_out, wout, w_sem.at[4]))
    for copy in weight_copies:
        copy.start()

    barrier = pltpu.get_barrier_semaphore()
    def greet(target):
        pl.semaphore_signal(barrier, inc=1, device_id=target, device_id_type=MESH)

    for q in range(NEAR):
        for k in range(8):
            if q or k:
                greet(device(z + group_dz(q), x + k // 2, c + k % 2, y))
    for dy in (1, 2, 3):
        for k in range(8):
            greet(device(z, x + k // 2, c + k % 2, y + dy))
    greet(device(z + 3, x, c, y))
    greet(device(z + 5, x, c, y))

    ids = jnp.concatenate([wanted[0:1, :], wanted[1:2, :]], axis=1)
    pick_high = (iota((128, CANDS), 0) == (ids >> 7)).astype(BF16)
    slots_2d = item_slot[...]
    at_high = dot_tn((slots_2d >> 7).astype(F32).astype(BF16), pick_high) * 128.0 + dot_tn(
        (slots_2d & 127).astype(F32).astype(BF16), pick_high
    )
    slot = jnp.sum(jnp.where(iota((128, CANDS), 0) == (ids & 127), at_high, 0.0), axis=0, keepdims=True)
    slot = slot.astype(I32)
    owner, local = slot >> 8, slot & 255
    dz = ((owner >> 3) - z) & 7
    dx = (((owner >> 1) & 3) - x) & 3
    dc = (owner - c) & 1
    lot = group_of_dz(dz) * 8 + dx * 2 + dc
    is_lot = iota((OWNERS, CANDS), 0) == lot
    lot_hot = is_lot.astype(BF16)
    earlier = (iota((CANDS, CANDS), 0) < iota((CANDS, CANDS), 1)).astype(BF16)
    before = dot(lot_hot, earlier)
    rank = jnp.sum(jnp.where(is_lot, before, 0.0), axis=0, keepdims=True).astype(I32)
    lane = (lot & 7) * CAP + rank
    lane_local = jnp.where(iota((128, CANDS), 0) == lane, local, 0).astype(F32).astype(BF16)
    request_rows = dot_nt(lot_hot, lane_local).astype(I32)
    for j in range(OWNERS):
        requests[j] = request_rows[j : j + 1, :]
    asked[0] = request_rows[0:1, :]

    normed[y] = layer_norm(tokens[...].astype(F32), gain_in[...]).astype(BF16)

    pl.semaphore_wait(barrier, 65)

    for q in range(8):
        dz = group_dz(q)
        if q < NEAR:
            for k in range(8):
                if q or k:
                    j = q * 8 + k
                    remote(
                        requests.at[j], asked.at[j], req_send, req_recv.at[q],
                        device(z + dz, x + k // 2, c + k % 2, y),
                    ).start()
        else:
            holder_y = (z + dz) % 4
            for k in range(8):
                j = q * 8 + k

                def ask(j=j, k=k, holder_y=holder_y, dz=dz):
                    remote(
                        requests.at[j], asked_far.at[y * 8 + k], req_send, far_req_recv,
                        device(z, x + k // 2, c + k % 2, holder_y),
                    ).start()

                if k:
                    ask()
                else:
                    pl.when(holder_y != y)(ask)

                    @pl.when(holder_y == y)
                    def _(j=j):
                        asked_far[y * 8] = requests[j]

    phase = (z + 8 - y) % 4
    is_holder = phase != 2
    first_half, last_half = pl.ds(0, ROWS // 2), pl.ds(ROWS // 2, ROWS // 2)
    z_up, z_down = device(z + 1, x, c, y), device(z - 1, x, c, y)

    @pl.when(phase == 0)
    def _():
        far_up, far_down = device(z + 3, x, c, y), device(z - 3, x, c, y)
        remote(table.at[first_half], far_table.at[first_half], copy_up, copy_recv.at[0], far_up).start()
        remote(table.at[last_half], far_table.at[last_half], copy_down, copy_recv.at[0], far_down).start()
        remote(table.at[last_half], far_table.at[last_half], copy_up, copy_recv.at[1], far_up).start()
        remote(table.at[first_half], far_table.at[first_half], copy_down, copy_recv.at[1], far_down).start()

    up = device(z, x, c, y + 1)
    own = normed.at[y]
    for dy in (1, 3, 2):
        remote(own, own, ring_send, ring_recv.at[dy - 1], device(z, x, c, y + dy)).start()

    place[:, 0:1] = jnp.sum(
        jnp.where(iota((CANDS, CANDS), 0) == iota((CANDS, CANDS), 1), lot * CAP + rank, 0).astype(F32),
        axis=1,
        keepdims=True,
    ).astype(I32)

    def gather(source, ask, first):
        gathered = ask[first]
        for k in range(1, 8):
            gathered = gathered + ask[first + k]
        pick = (iota((ROWS, CHUNK), 0) == gathered).astype(BF16)
        return dot_tn(pick, source[...]).astype(BF16)

    def send_near(q, k):
        rows = pl.ds(q * CHUNK + k * CAP, CAP)
        remote(
            served.at[rows], embedded.at[rows], row_send, row_recv.at[q],
            device(z - group_dz(q), x - k // 2, c - k % 2, y),
        ).start()

    for q in range(NEAR):
        first = 1 if q == 0 else 0
        lots = pl.ds(q * 8 + first, 8 - first)
        remote(asked.at[lots], asked.at[lots], req_send, req_recv.at[q], up).wait_recv()
        served[pl.ds(q * CHUNK, CHUNK), :] = gather(table, asked, q * 8)
        if q == 0:
            for k in range(1, 8):
                send_near(0, k)
            embedded[pl.ds(0, CAP), :] = served[pl.ds(0, CAP), :]

    @pl.when(phase == 3)
    def _():
        half = far_table.at[first_half]
        remote(half, half, copy_up, copy_recv.at[0], z_up).wait_recv()
        remote(half, half, copy_up, copy_recv.at[0], z_up).start()

    @pl.when(phase == 1)
    def _():
        half = far_table.at[last_half]
        remote(half, half, copy_down, copy_recv.at[0], z_down).wait_recv()
        remote(half, half, copy_down, copy_recv.at[1], z_down).start()

    def project(rows_value, block, write):
        def step(n, carry):
            columns = pl.ds(pl.multiple_of(n * 256, 256), 256)
            write(columns, dot(rows_value(), win[block, :, columns]))
            return carry

        lax.fori_loop(0, WIDTH // 256, step, 0)

    def project_keys(block):
        rows = pl.ds(pl.multiple_of(block * ROWS, ROWS), ROWS)

        def write_value(columns, out):
            values[rows, columns] = out.astype(BF16)

        def write_key(columns, out):
            keys[rows, columns] = out.astype(BF16)

        project(lambda: normed[block], 1, write_value)
        project(lambda: normed[block], 3, write_key)

    def write_hgate(columns, out):
        hgate[:, columns] = half_silu(out * 0.5).astype(BF16)

    def write_hquery(columns, out):
        hquery[:, columns] = out.astype(BF16)

    for copy in weight_copies:
        copy.wait()
    project(lambda: normed[y], 0, write_hgate)
    project(lambda: normed[y], 2, write_hquery)
    project_keys(y)

    @pl.when(phase == 0)
    def _():
        half, other = far_table.at[first_half], far_table.at[last_half]
        remote(half, half, copy_up, copy_recv.at[0], z_up).wait_recv()
        remote(other, other, copy_up, copy_recv.at[1], z_up).wait_recv()

    @pl.when(phase % 2 == 1)
    def _():
        half = far_table.at[first_half]
        remote(half, half, copy_up, copy_recv.at[1], z_up).wait_recv()

    far_group = jnp.where(phase == 0, 7, jnp.where(phase == 3, 6, 5))
    far_base = pl.multiple_of(far_group * CHUNK, CHUNK)

    @pl.when(is_holder)
    def _():
        lots = asked_far.at[pl.ds(0, 31)]
        remote(lots, lots, req_send, far_req_recv, up).wait_recv()
        for dy in range(4):
            served_far[pl.ds(dy * CHUNK, CHUNK), :] = gather(far_table, asked_far, (y + dy) % 4 * 8)
        embedded[pl.ds(far_base, CAP), :] = served_far[0:CAP, :]

    for k in range(8):
        for q in range(1, NEAR):
            send_near(q, k)
            dy = q - 1
            if dy or k:

                @pl.when(is_holder)
                def _(dy=dy, k=k):
                    remote(
                        served_far.at[pl.ds(dy * CHUNK + k * CAP, CAP)],
                        embedded.at[pl.ds(pl.multiple_of(far_base + k * CAP, CAP), CAP)],
                        far_row_send, row_recv.at[far_group],
                        device(z, x - k // 2, c - k % 2, y + dy),
                    ).start()

    for dy in (1, 3, 2):
        block = (y - dy + 4) % 4
        remote(normed.at[block], normed.at[block], ring_send, ring_recv.at[dy - 1], up).wait_recv()
        project_keys(block)

    def emit(source, target, index):
        copy = pltpu.make_async_copy(source, target, out_sem.at[index])
        copy.start()
        return copy

    emitted = [emit(keys, keys_done, 0), emit(values, values_done, 1)]

    group_base = me * KEYS
    second = row_start[1] - group_base
    end_first, end_second = row_start[0] - group_base + hist_len[0], second + hist_len[1]

    def locate(spot):
        user = (spot >= second).astype(I32)
        return user, spot < jnp.where(user == 1, end_second, end_first)

    key_spot = iota((1, KEYS), 1)
    key_user, key_live = locate(key_spot)
    query_spot = y * ROWS + iota((ROWS, 1), 0)
    query_user, query_live = locate(query_spot)

    def attend(rows, query):
        def head(h, carry):
            columns = pl.ds(pl.multiple_of(h * HEAD_DIM, HEAD_DIM), HEAD_DIM)
            scores = dot_nt(query[:, columns], keys[:, columns])
            weights = half_silu(scores * scale_mask[0:rows, :]).astype(BF16)
            attended[0:rows, columns] = dot(weights, values[:, columns])
            return carry

        lax.fori_loop(0, HEADS, head, 0, unroll=4)

    def finish(rows, residual, gate, write):
        mixed = (layer_norm(attended[0:rows, :], gain_attn[...]) * gate[...].astype(F32)).astype(BF16)
        for n in range(WIDTH // 256):
            columns = pl.ds(n * 256, 256)
            write(columns, (residual(columns) + dot(mixed, wout[:, columns])).astype(BF16))

    allowed = (
        (query_user == key_user)
        & (query_live & key_live)
        & (key_spot <= query_spot)
    )
    scale_mask[...] = jnp.where(allowed, half_scale, 0.0)
    attend(ROWS, hquery)

    def write_hist(columns, out):
        hist[:, columns] = out

    finish(ROWS, lambda columns: tokens[:, columns].astype(F32), hgate, write_hist)

    emitted.append(emit(hist, hist_done, 2))

    def pick_rows(first, count):
        def part(n, carry):
            rows = pl.ds(pl.multiple_of(n * 256, 256), 256)
            pick = (iota((256, count), 1) + first == place[rows, 0:1]).astype(BF16)
            for m in range(WIDTH // 256):
                columns = pl.ds(m * 256, 256)
                found = dot(pick, embedded[pl.ds(first, count), columns])
                if first:
                    found = found + rows_in[rows, columns]
                rows_in[rows, columns] = found
            return carry

        lax.fori_loop(0, CANDS // 256, part, 0)

    for q in range(NEAR):
        rows = pl.ds(CAP, CHUNK - CAP) if q == 0 else pl.ds(q * CHUNK, CHUNK)
        remote(embedded.at[rows], embedded.at[rows], row_send, row_recv.at[q], up).wait_recv()
    pick_rows(0, NEAR * CHUNK)
    for q in range(NEAR, 8):
        own_copy = (z + group_dz(q)) % 4 == y

        @pl.when(own_copy)
        def _(q=q):
            rows = pl.ds(q * CHUNK + CAP, CHUNK - CAP)
            remote(embedded.at[rows], embedded.at[rows], row_send, row_recv.at[q], up).wait_recv()

        @pl.when(jnp.logical_not(own_copy))
        def _(q=q):
            rows = pl.ds(q * CHUNK, CHUNK)
            remote(embedded.at[rows], embedded.at[rows], row_send, row_recv.at[q], up).wait_recv()

    pick_rows(NEAR * CHUNK, (8 - NEAR) * CHUNK)

    def norm_rows(n, carry):
        rows = pl.ds(pl.multiple_of(n * CHUNK, CHUNK), CHUNK)
        value = rows_in[rows, :]
        rows_out[rows, :] = value.astype(BF16)
        cnormed[rows, :] = layer_norm(value, gain_in[...]).astype(BF16)
        return carry

    lax.fori_loop(0, CANDS // CHUNK, norm_rows, 0)
    emitted.append(emit(rows_out, rows_done, 3))

    def write_cquery(columns, out):
        cquery[:, columns] = out.astype(BF16)

    def write_cgate(columns, out):
        cgate[:, columns] = half_silu(out * 0.5).astype(BF16)

    project(lambda: cnormed[...], 2, write_cquery)
    emitted.append(emit(cquery, query_done, 4))
    project(lambda: cnormed[...], 0, write_cgate)
    emitted.append(emit(cgate, gate_done, 5))

    others = normed.at[pl.ds(0, 3)]
    remote(others, others, ring_send, ring_recv.at[0], up).wait_send()
    lots = requests.at[pl.ds(0, OWNERS - 2)]
    remote(lots, lots, req_send, req_recv.at[0], up).wait_send()

    @pl.when(jnp.logical_not(is_holder))
    def _():
        remote(requests.at[0], requests.at[0], req_send, req_recv.at[0], up).wait_send()

    rows = served.at[pl.ds(CAP, NEAR * CHUNK - CAP)]
    remote(rows, rows, row_send, row_recv.at[0], up).wait_send()

    @pl.when(is_holder)
    def _():
        rows = served_far.at[pl.ds(CAP, 4 * CHUNK - CAP)]
        remote(rows, rows, far_row_send, row_recv.at[0], up).wait_send()

    @pl.when(phase == 0)
    def _():
        remote(far_table, far_table, copy_up, copy_recv.at[0], z_up).wait_send()
        remote(far_table, far_table, copy_down, copy_recv.at[0], z_down).wait_send()

    @pl.when(phase == 3)
    def _():
        half = far_table.at[first_half]
        remote(half, half, copy_up, copy_recv.at[0], z_up).wait_send()

    @pl.when(phase == 1)
    def _():
        half = far_table.at[last_half]
        remote(half, half, copy_down, copy_recv.at[0], z_down).wait_send()

    for copy in emitted:
        copy.wait()


def candidate_kernel(
    hist_len, row_start, base, hist, keys_in, values_in, rows_in, gate_in, query_in, w_out, gain_attn,
    hist_out, cand_out,
    keys, values, rows, gate, query, wout, attended, result, hist_held, sem, out_sem,
):
    half_scale = 0.5 / math.sqrt(HEAD_DIM)
    hist_copy = pltpu.make_async_copy(hist, hist_held, sem.at[6])
    loads = [
        pltpu.make_async_copy(source, target, sem.at[n])
        for n, (source, target) in enumerate(
            [(query_in, query), (keys_in, keys), (values_in, values), (gate_in, gate), (w_out, wout), (rows_in, rows)]
        )
    ]
    for copy in loads:
        copy.start()
    hist_copy.start()
    second = row_start[1] - base[0]
    starts = (0, second)
    ends = (row_start[0] - base[0] + hist_len[0], second + hist_len[1])
    tiles = ((0, (second + 255) // 256), (second // 256, KEYS // 256))
    stores = []
    for copy in loads[:3]:
        copy.wait()
    for user in range(2):
        own = pl.ds(user * 256, 256)
        attended[...] = jnp.zeros_like(attended)

        def tile(t, carry, user=user, own=own):
            first = pl.multiple_of(t * 256, 256)
            spot = first + iota((1, 256), 1)
            live = (spot >= starts[user]) & (spot < ends[user])
            scale = jnp.where(live, half_scale, 0.0)
            span = pl.ds(first, 256)
            for h in range(HEADS):
                columns = pl.ds(h * HEAD_DIM, HEAD_DIM)
                scores = dot_nt(query[own, columns], keys[span, columns])
                weights = half_silu(scores * scale).astype(BF16)
                attended[:, columns] += dot(weights, values[span, columns])
            return carry

        lax.fori_loop(tiles[user][0], tiles[user][1], tile, 0)
        if user == 0:
            for copy in loads[3:]:
                copy.wait()
            hist_copy.wait()
            stores.append(pltpu.make_async_copy(hist_held, hist_out, out_sem.at[2]))
            stores[-1].start()
        mixed = (layer_norm(attended[...], gain_attn[...]) * gate[own, :].astype(F32)).astype(BF16)
        for n in range(WIDTH // 256):
            columns = pl.ds(n * 256, 256)
            result[user, :, columns] = (
                rows[own, columns].astype(F32) + dot(mixed, wout[:, columns])
            ).astype(BF16)
        stores.append(pltpu.make_async_copy(result.at[user], cand_out.at[user], out_sem.at[user]))
        stores[-1].start()
    for copy in stores:
        copy.wait()


def body(
    tokens, item_table, w_in, w_out, gain_in, gain_attn, hist_len, row_start, impressions, item_slot
):
    vmem = pl.BlockSpec(memory_space=pltpu.VMEM)
    smem = pl.BlockSpec(memory_space=pltpu.SMEM)
    anywhere = pl.BlockSpec(memory_space=pl.ANY)
    gain_attn_row = gain_attn.reshape(1, WIDTH)
    big = jax.ShapeDtypeStruct((KEYS, WIDTH), BF16)
    half = jax.ShapeDtypeStruct((CANDS, WIDTH), BF16)
    hist, keys, values, rows, gate, query = pl.pallas_call(
        kernel,
        out_shape=(jax.ShapeDtypeStruct((ROWS, WIDTH), BF16), big, big, half, half, half),
        in_specs=[smem, smem, vmem, vmem, anywhere, anywhere, vmem, vmem, vmem, vmem],
        out_specs=(anywhere,) * 6,
        scratch_shapes=[
            pltpu.VMEM((4, WIDTH, WIDTH), BF16),
            pltpu.VMEM((WIDTH, WIDTH), BF16),
            pltpu.VMEM((4, ROWS, WIDTH), BF16),
            pltpu.VMEM((KEYS, WIDTH), BF16),
            pltpu.VMEM((KEYS, WIDTH), BF16),
            pltpu.VMEM((ROWS, WIDTH), BF16),
            pltpu.VMEM((ROWS, WIDTH), BF16),
            pltpu.VMEM((ROWS, WIDTH), F32),
            pltpu.VMEM((ROWS, KEYS), F32),
            pltpu.VMEM((ROWS, WIDTH), BF16),
            pltpu.VMEM((OWNERS, 1, 128), I32),
            pltpu.VMEM((NEAR * 8, 1, 128), I32),
            pltpu.VMEM((32, 1, 128), I32),
            pltpu.VMEM((ROWS, WIDTH), BF16),
            pltpu.VMEM((NEAR * CHUNK, WIDTH), BF16),
            pltpu.VMEM((4 * CHUNK, WIDTH), BF16),
            pltpu.VMEM((OWNERS * CAP, WIDTH), BF16),
            pltpu.VMEM((CANDS, WIDTH), F32),
            pltpu.VMEM((CANDS, WIDTH), BF16),
            pltpu.VMEM((CANDS, WIDTH), BF16),
            pltpu.VMEM((CANDS, WIDTH), BF16),
            pltpu.VMEM((CANDS, WIDTH), BF16),
            pltpu.VMEM((CANDS, 128), I32),
            pltpu.SemaphoreType.DMA((5,)),
            pltpu.SemaphoreType.DMA,
            pltpu.SemaphoreType.DMA((NEAR,)),
            pltpu.SemaphoreType.DMA,
            pltpu.SemaphoreType.DMA,
            pltpu.SemaphoreType.DMA,
            pltpu.SemaphoreType.DMA((8,)),
            pltpu.SemaphoreType.DMA,
            pltpu.SemaphoreType.DMA((3,)),
            pltpu.SemaphoreType.DMA,
            pltpu.SemaphoreType.DMA,
            pltpu.SemaphoreType.DMA((2,)),
            pltpu.SemaphoreType.DMA((6,)),
        ],
        compiler_params=pltpu.CompilerParams(
            collective_id=0, has_side_effects=True, vmem_limit_bytes=56 * 2**20
        ),
    )(
        hist_len, row_start, tokens, item_table, w_in, w_out,
        gain_in.reshape(1, WIDTH), gain_attn_row,
        impressions, item_slot.reshape(128, 128),
    )
    base = (lax.axis_index("users") * KEYS).astype(I32).reshape(1)
    return pl.pallas_call(
        candidate_kernel,
        out_shape=(
            jax.ShapeDtypeStruct((ROWS, WIDTH), BF16),
            jax.ShapeDtypeStruct((2, CANDS // 2, WIDTH), BF16),
        ),
        in_specs=[smem, smem, smem] + [anywhere] * 7 + [vmem],
        out_specs=(anywhere, anywhere),
        scratch_shapes=[
            pltpu.VMEM((KEYS, WIDTH), BF16),
            pltpu.VMEM((KEYS, WIDTH), BF16),
            pltpu.VMEM((CANDS, WIDTH), BF16),
            pltpu.VMEM((CANDS, WIDTH), BF16),
            pltpu.VMEM((CANDS, WIDTH), BF16),
            pltpu.VMEM((WIDTH, WIDTH), BF16),
            pltpu.VMEM((CANDS // 2, WIDTH), F32),
            pltpu.VMEM((2, CANDS // 2, WIDTH), BF16),
            pltpu.VMEM((ROWS, WIDTH), BF16),
            pltpu.SemaphoreType.DMA((7,)),
            pltpu.SemaphoreType.DMA((3,)),
        ],
        compiler_params=pltpu.CompilerParams(vmem_limit_bytes=56 * 2**20),
    )(hist_len, row_start, base, hist, keys, values, rows, gate, query, w_out, gain_attn_row)


def solution(mesh):
    placed = (
        P(("users", "seq"), None),
        P("users", None),
        P(),
        P(),
        P(),
        P(),
        P("users"),
        P("users"),
        P("users", "seq"),
        P(),
    )
    return jax.shard_map(
        body,
        mesh=mesh,
        in_specs=placed,
        out_specs=(P(("users", "seq"), None), P("users", "seq", None)),
        check_vma=False,
    )
```

```python
import functools
import math

import jax
import jax.numpy as jnp
from jax import lax
from jax.experimental import pallas as pl
from jax.experimental.pallas import tpu as pltpu
from jax.sharding import PartitionSpec as P

MESH = pl.DeviceIdType.MESH
HEADS = 8
WIDTH = 1024
HEAD_DIM = WIDTH // HEADS
ROWS = 256
CANDS = 512
KEYS = 1024
CAP = 16
OWNERS = 64
NEAR = 5
CHUNK = 128
epsilon = 1e-05
F32 = jnp.float32
BF16 = jnp.bfloat16
I32 = jnp.int32


def group_dz(q):
    return [0, 1, 7, 2, 6, 3, 5, 4][q]


def group_of_dz(dz):
    return jnp.where(dz == 0, 0, jnp.where(dz <= 4, 2 * dz - 1, 2 * (8 - dz)))


def layer_norm(values, gain_row):
    centered = values - jnp.mean(values, axis=-1, keepdims=True)
    spread = jnp.mean(centered * centered, axis=-1, keepdims=True)
    return centered * lax.rsqrt(spread + epsilon) * gain_row


def half_silu(half):
    return half + half * jnp.tanh(half)


def dot(a, b):
    return jnp.dot(a, b, preferred_element_type=F32)


def dot_nt(a, b):
    return lax.dot_general(a, b, (((1,), (1,)), ((), ())), preferred_element_type=F32)


def dot_tn(a, b):
    return lax.dot_general(a, b, (((0,), (0,)), ((), ())), preferred_element_type=F32)


def iota(shape, dim):
    return lax.broadcasted_iota(I32, shape, dim)


def kernel(
    hist_len, row_start, tokens, table, w_in, w_out, gain_in, gain_attn, wanted, item_slot,
    hist_done, rows_done, mixed_done,
    win, wout, normed, keys, values, hgate, hquery, attended, scale_mask, hist,
    requests, asked, asked_far, far_table, served, served_far, embedded,
    rows_in, rows_out, cnormed, cgate, cquery, cattended, cmixed, place,
    w_sem, req_send, req_recv, far_req_recv, row_send, far_row_send, row_recv,
    ring_send, ring_recv, copy_up, copy_down, copy_recv, out_sem,
):
    me = lax.axis_index("users")
    y = lax.axis_index("seq")
    z, x, c = me // 8, (me // 2) % 4, me % 2
    half_scale = 0.5 / math.sqrt(HEAD_DIM)

    def device(zz, xx, cc, yy):
        return {"users": ((zz + 8) % 8) * 8 + ((xx + 4) % 4) * 2 + (cc + 2) % 2, "seq": (yy + 4) % 4}

    def remote(src, dst, send, recv, target):
        return pltpu.make_async_remote_copy(
            src_ref=src, dst_ref=dst, send_sem=send, recv_sem=recv, device_id=target, device_id_type=MESH
        )

    weight_copies = [
        pltpu.make_async_copy(w_in.at[:, pl.ds(b * WIDTH, WIDTH)], win.at[b], w_sem.at[b]) for b in range(4)
    ]
    weight_copies.append(pltpu.make_async_copy(w_out, wout, w_sem.at[4]))
    for copy in weight_copies:
        copy.start()

    barrier = pltpu.get_barrier_semaphore()
    def greet(target):
        pl.semaphore_signal(barrier, inc=1, device_id=target, device_id_type=MESH)

    for q in range(NEAR):
        for k in range(8):
            if q or k:
                greet(device(z + group_dz(q), x + k // 2, c + k % 2, y))
    for dy in (1, 2, 3):
        for k in range(8):
            greet(device(z, x + k // 2, c + k % 2, y + dy))
    greet(device(z + 3, x, c, y))
    greet(device(z + 5, x, c, y))

    ids = jnp.concatenate([wanted[0:1, :], wanted[1:2, :]], axis=1)
    pick_high = (iota((128, CANDS), 0) == (ids >> 7)).astype(BF16)
    slots_2d = item_slot[...]
    at_high = dot_tn((slots_2d >> 7).astype(F32).astype(BF16), pick_high) * 128.0 + dot_tn(
        (slots_2d & 127).astype(F32).astype(BF16), pick_high
    )
    slot = jnp.sum(jnp.where(iota((128, CANDS), 0) == (ids & 127), at_high, 0.0), axis=0, keepdims=True)
    slot = slot.astype(I32)
    owner, local = slot >> 8, slot & 255
    dz = ((owner >> 3) - z) & 7
    dx = (((owner >> 1) & 3) - x) & 3
    dc = (owner - c) & 1
    lot = group_of_dz(dz) * 8 + dx * 2 + dc
    is_lot = iota((OWNERS, CANDS), 0) == lot
    lot_hot = is_lot.astype(BF16)
    earlier = (iota((CANDS, CANDS), 0) < iota((CANDS, CANDS), 1)).astype(BF16)
    before = dot(lot_hot, earlier)
    rank = jnp.sum(jnp.where(is_lot, before, 0.0), axis=0, keepdims=True).astype(I32)
    lane = (lot & 7) * CAP + rank
    lane_local = jnp.where(iota((128, CANDS), 0) == lane, local, 0).astype(F32).astype(BF16)
    request_rows = dot_nt(lot_hot, lane_local).astype(I32)
    for j in range(OWNERS):
        requests[j] = request_rows[j : j + 1, :]
    asked[0] = request_rows[0:1, :]

    pl.semaphore_wait(barrier, 65)

    for q in range(8):
        dz = group_dz(q)
        if q < NEAR:
            for k in range(8):
                if q or k:
                    j = q * 8 + k
                    remote(
                        requests.at[j], asked.at[j], req_send, req_recv.at[q],
                        device(z + dz, x + k // 2, c + k % 2, y),
                    ).start()
        else:
            holder_y = (z + dz) % 4
            for k in range(8):
                j = q * 8 + k

                def ask(j=j, k=k, holder_y=holder_y, dz=dz):
                    remote(
                        requests.at[j], asked_far.at[y * 8 + k], req_send, far_req_recv,
                        device(z, x + k // 2, c + k % 2, holder_y),
                    ).start()

                if k:
                    ask()
                else:
                    pl.when(holder_y != y)(ask)

                    @pl.when(holder_y == y)
                    def _(j=j):
                        asked_far[y * 8] = requests[j]

    phase = (z + 8 - y) % 4
    is_holder = phase != 2
    first_half, last_half = pl.ds(0, ROWS // 2), pl.ds(ROWS // 2, ROWS // 2)
    z_up, z_down = device(z + 1, x, c, y), device(z - 1, x, c, y)

    @pl.when(phase == 0)
    def _():
        far_up, far_down = device(z + 3, x, c, y), device(z - 3, x, c, y)
        remote(table.at[first_half], far_table.at[first_half], copy_up, copy_recv.at[0], far_up).start()
        remote(table.at[last_half], far_table.at[last_half], copy_down, copy_recv.at[0], far_down).start()
        remote(table.at[last_half], far_table.at[last_half], copy_up, copy_recv.at[1], far_up).start()
        remote(table.at[first_half], far_table.at[first_half], copy_down, copy_recv.at[1], far_down).start()

    up = device(z, x, c, y + 1)
    own = normed.at[y]
    normed[y] = layer_norm(tokens[...].astype(F32), gain_in[...]).astype(BF16)
    for dy in (1, 3, 2):
        remote(own, own, ring_send, ring_recv.at[dy - 1], device(z, x, c, y + dy)).start()

    place[:, 0:1] = jnp.sum(
        jnp.where(iota((CANDS, CANDS), 0) == iota((CANDS, CANDS), 1), lot * CAP + rank, 0).astype(F32),
        axis=1,
        keepdims=True,
    ).astype(I32)

    def gather(source, ask, first):
        gathered = ask[first]
        for k in range(1, 8):
            gathered = gathered + ask[first + k]
        pick = (iota((ROWS, CHUNK), 0) == gathered).astype(BF16)
        return dot_tn(pick, source[...]).astype(BF16)

    def send_near(q, k):
        rows = pl.ds(q * CHUNK + k * CAP, CAP)
        remote(
            served.at[rows], embedded.at[rows], row_send, row_recv.at[q],
            device(z - group_dz(q), x - k // 2, c - k % 2, y),
        ).start()

    for q in range(NEAR):
        first = 1 if q == 0 else 0
        lots = pl.ds(q * 8 + first, 8 - first)
        remote(asked.at[lots], asked.at[lots], req_send, req_recv.at[q], up).wait_recv()
        served[pl.ds(q * CHUNK, CHUNK), :] = gather(table, asked, q * 8)
        if q == 0:
            for k in range(1, 8):
                send_near(0, k)
            embedded[pl.ds(0, CAP), :] = served[pl.ds(0, CAP), :]

    @pl.when(phase == 3)
    def _():
        half = far_table.at[first_half]
        remote(half, half, copy_up, copy_recv.at[0], z_up).wait_recv()
        remote(half, half, copy_up, copy_recv.at[0], z_up).start()

    @pl.when(phase == 1)
    def _():
        half = far_table.at[last_half]
        remote(half, half, copy_down, copy_recv.at[0], z_down).wait_recv()
        remote(half, half, copy_down, copy_recv.at[1], z_down).start()

    def project(rows_value, block, write):
        def step(n, carry):
            columns = pl.ds(pl.multiple_of(n * 256, 256), 256)
            write(columns, dot(rows_value(), win[block, :, columns]))
            return carry

        lax.fori_loop(0, WIDTH // 256, step, 0, unroll=4)

    def project_keys(block):
        rows = pl.ds(pl.multiple_of(block * ROWS, ROWS), ROWS)

        def write_value(columns, out):
            values[rows, columns] = out.astype(BF16)

        def write_key(columns, out):
            keys[rows, columns] = out.astype(BF16)

        project(lambda: normed[block], 1, write_value)
        project(lambda: normed[block], 3, write_key)

    def write_hgate(columns, out):
        hgate[:, columns] = half_silu(out * 0.5).astype(BF16)

    def write_hquery(columns, out):
        hquery[:, columns] = out.astype(BF16)

    for copy in weight_copies:
        copy.wait()
    project(lambda: normed[y], 0, write_hgate)
    project(lambda: normed[y], 2, write_hquery)
    project_keys(y)

    @pl.when(phase == 0)
    def _():
        half, other = far_table.at[first_half], far_table.at[last_half]
        remote(half, half, copy_up, copy_recv.at[0], z_up).wait_recv()
        remote(other, other, copy_up, copy_recv.at[1], z_up).wait_recv()

    @pl.when(phase % 2 == 1)
    def _():
        half = far_table.at[first_half]
        remote(half, half, copy_up, copy_recv.at[1], z_up).wait_recv()

    far_group = jnp.where(phase == 0, 7, jnp.where(phase == 3, 6, 5))
    far_base = pl.multiple_of(far_group * CHUNK, CHUNK)

    @pl.when(is_holder)
    def _():
        lots = asked_far.at[pl.ds(0, 31)]
        remote(lots, lots, req_send, far_req_recv, up).wait_recv()
        for dy in range(4):
            served_far[pl.ds(dy * CHUNK, CHUNK), :] = gather(far_table, asked_far, (y + dy) % 4 * 8)
        embedded[pl.ds(far_base, CAP), :] = served_far[0:CAP, :]

    for k in range(8):
        for q in range(1, NEAR):
            send_near(q, k)
            dy = q - 1
            if dy or k:

                @pl.when(is_holder)
                def _(dy=dy, k=k):
                    remote(
                        served_far.at[pl.ds(dy * CHUNK + k * CAP, CAP)],
                        embedded.at[pl.ds(pl.multiple_of(far_base + k * CAP, CAP), CAP)],
                        far_row_send, row_recv.at[far_group],
                        device(z, x - k // 2, c - k % 2, y + dy),
                    ).start()

    for dy in (1, 3, 2):
        block = (y - dy + 4) % 4
        remote(normed.at[block], normed.at[block], ring_send, ring_recv.at[dy - 1], up).wait_recv()
        project_keys(block)

    def emit(source, target, index):
        copy = pltpu.make_async_copy(source, target, out_sem.at[index])
        copy.start()
        return copy

    emitted = []

    group_base = me * KEYS
    second = row_start[1] - group_base
    end_first, end_second = row_start[0] - group_base + hist_len[0], second + hist_len[1]

    def locate(spot):
        user = (spot >= second).astype(I32)
        return user, spot < jnp.where(user == 1, end_second, end_first)

    key_spot = iota((1, KEYS), 1)
    key_user, key_live = locate(key_spot)
    query_spot = y * ROWS + iota((ROWS, 1), 0)
    query_user, query_live = locate(query_spot)

    def attend(rows, query):
        def head(h, carry):
            columns = pl.ds(pl.multiple_of(h * HEAD_DIM, HEAD_DIM), HEAD_DIM)
            scores = dot_nt(query[:, columns], keys[:, columns])
            weights = half_silu(scores * scale_mask[0:rows, :]).astype(BF16)
            attended[0:rows, columns] = dot(weights, values[:, columns])
            return carry

        lax.fori_loop(0, HEADS, head, 0, unroll=4)

    def finish(rows, residual, gate, write):
        mixed = (layer_norm(attended[0:rows, :], gain_attn[...]) * gate[...].astype(F32)).astype(BF16)
        for n in range(WIDTH // 256):
            columns = pl.ds(n * 256, 256)
            write(columns, (residual(columns) + dot(mixed, wout[:, columns])).astype(BF16))

    allowed = (
        (query_user == key_user)
        & (query_live & key_live)
        & (key_spot <= query_spot)
    )
    scale_mask[...] = jnp.where(allowed, half_scale, 0.0)
    attend(ROWS, hquery)

    def write_hist(columns, out):
        hist[:, columns] = out

    finish(ROWS, lambda columns: tokens[:, columns].astype(F32), hgate, write_hist)

    emitted.append(emit(hist, hist_done, 0))

    def pick_rows(first, count):
        def part(n, carry):
            rows = pl.ds(pl.multiple_of(n * 256, 256), 256)
            pick = (iota((256, count), 1) + first == place[rows, 0:1]).astype(BF16)
            for m in range(WIDTH // 256):
                columns = pl.ds(m * 256, 256)
                found = dot(pick, embedded[pl.ds(first, count), columns])
                if first:
                    found = found + rows_in[rows, columns]
                rows_in[rows, columns] = found
            return carry

        lax.fori_loop(0, CANDS // 256, part, 0)

    for q in range(NEAR):
        rows = pl.ds(CAP, CHUNK - CAP) if q == 0 else pl.ds(q * CHUNK, CHUNK)
        remote(embedded.at[rows], embedded.at[rows], row_send, row_recv.at[q], up).wait_recv()
    pick_rows(0, NEAR * CHUNK)
    for q in range(NEAR, 8):
        own_copy = (z + group_dz(q)) % 4 == y

        @pl.when(own_copy)
        def _(q=q):
            rows = pl.ds(q * CHUNK + CAP, CHUNK - CAP)
            remote(embedded.at[rows], embedded.at[rows], row_send, row_recv.at[q], up).wait_recv()

        @pl.when(jnp.logical_not(own_copy))
        def _(q=q):
            rows = pl.ds(q * CHUNK, CHUNK)
            remote(embedded.at[rows], embedded.at[rows], row_send, row_recv.at[q], up).wait_recv()

    pick_rows(NEAR * CHUNK, (8 - NEAR) * CHUNK)

    def norm_rows(n, carry):
        rows = pl.ds(pl.multiple_of(n * CHUNK, CHUNK), CHUNK)
        value = rows_in[rows, :]
        rows_out[rows, :] = value.astype(BF16)
        cnormed[rows, :] = layer_norm(value, gain_in[...]).astype(BF16)
        return carry

    lax.fori_loop(0, CANDS // CHUNK, norm_rows, 0)
    emitted.append(emit(rows_out, rows_done, 1))

    def write_cquery(columns, out):
        cquery[:, columns] = out.astype(BF16)

    def write_cgate(columns, out):
        cgate[:, columns] = half_silu(out * 0.5).astype(BF16)

    project(lambda: cnormed[...], 2, write_cquery)

    lanes = iota((1, HEAD_DIM), 1)
    tile_lanes = iota((1, 256), 1)
    to_second = [(lanes * 0 + t * 256 >= second).astype(F32) for t in range(4)]
    to_first = [(lanes * 0 + t * 256 < second).astype(F32) for t in range(4)]
    shared = second >> 8
    is_shared = [(lanes * 0 + t == shared).astype(F32).astype(BF16) for t in range(4)]

    def tile_scale(spot, second_rows):
        low = jnp.where(second_rows, second, 0)
        high = jnp.where(second_rows, end_second, end_first)
        return jnp.where((spot >= low) & (spot < high), half_scale, 0.0)

    scales = [tile_scale(tile_lanes + t * 256, tile_lanes * 0 + t * 256 >= second) for t in range(4)]
    shared_spot = tile_lanes + shared * 256
    shared_live = (shared_spot >= second) & (shared_spot < end_second) & (tile_lanes * 0 + shared * 256 < second)
    shared_scale = jnp.where(shared_live, half_scale, 0.0)

    def cand_head(h, carry):
        columns = pl.ds(pl.multiple_of(h * HEAD_DIM, HEAD_DIM), HEAD_DIM)
        first_query, second_query = cquery[0:256, columns], cquery[256:512, columns]

        def weigh(query, key, value, scale):
            return dot(half_silu(dot_nt(query, key) * scale).astype(BF16), value)

        key_shared = value_shared = None
        for t in range(4):
            span = pl.ds(t * 256, 256)
            key, value = keys[span, columns], values[span, columns]
            if t == 0:
                key_shared, value_shared = key * is_shared[t], value * is_shared[t]
                cattended[0:256, columns] = weigh(first_query, key, value, scales[t])
                continue
            key_shared = key_shared + key * is_shared[t]
            value_shared = value_shared + value * is_shared[t]
            query = first_query * to_first[t].astype(BF16) + second_query * to_second[t].astype(BF16)
            found = weigh(query, key, value, scales[t])
            cattended[0:256, columns] += found * to_first[t]
            if t == 1:
                cattended[256:512, columns] = found * to_second[t]
            else:
                cattended[256:512, columns] += found * to_second[t]
        cattended[256:512, columns] += weigh(second_query, key_shared, value_shared, shared_scale)
        return carry

    lax.fori_loop(0, HEADS, cand_head, 0, unroll=4)
    project(lambda: cnormed[...], 0, write_cgate)
    for n in range(4):
        rows = pl.ds(n * CHUNK, CHUNK)
        mixed = layer_norm(cattended[rows, :], gain_attn[...]) * cgate[rows, :].astype(F32)
        cmixed[rows, :] = mixed.astype(BF16)
        emitted.append(emit(cmixed.at[rows], mixed_done.at[rows], 2 + n))

    others = normed.at[pl.ds(0, 3)]
    remote(others, others, ring_send, ring_recv.at[0], up).wait_send()
    lots = requests.at[pl.ds(0, OWNERS - 2)]
    remote(lots, lots, req_send, req_recv.at[0], up).wait_send()

    @pl.when(jnp.logical_not(is_holder))
    def _():
        remote(requests.at[0], requests.at[0], req_send, req_recv.at[0], up).wait_send()

    rows = served.at[pl.ds(CAP, NEAR * CHUNK - CAP)]
    remote(rows, rows, row_send, row_recv.at[0], up).wait_send()

    @pl.when(is_holder)
    def _():
        rows = served_far.at[pl.ds(CAP, 4 * CHUNK - CAP)]
        remote(rows, rows, far_row_send, row_recv.at[0], up).wait_send()

    @pl.when(phase == 0)
    def _():
        remote(far_table, far_table, copy_up, copy_recv.at[0], z_up).wait_send()
        remote(far_table, far_table, copy_down, copy_recv.at[0], z_down).wait_send()

    @pl.when(phase == 3)
    def _():
        half = far_table.at[first_half]
        remote(half, half, copy_up, copy_recv.at[0], z_up).wait_send()

    @pl.when(phase == 1)
    def _():
        half = far_table.at[last_half]
        remote(half, half, copy_down, copy_recv.at[0], z_down).wait_send()

    for copy in emitted:
        copy.wait()


def output_kernel(
    hist, mixed_in, rows_in, w_out, hist_out, cand_out, wout, hist_held, mixed, rows, result, sem, out_sem
):
    def load(source, target, index):
        copy = pltpu.make_async_copy(source, target, sem.at[index])
        copy.start()
        return copy

    first_load = load(w_out, wout, 9)
    loads = []
    for n in range(4):
        part = pl.ds(n * CHUNK, CHUNK)
        loads.append(
            (load(mixed_in.at[part], mixed.at[part], 2 * n), load(rows_in.at[part], rows.at[part], 2 * n + 1))
        )
    hist_load = load(hist, hist_held, 8)
    stores = []

    def store(source, target, index):
        copy = pltpu.make_async_copy(source, target, out_sem.at[index])
        copy.start()
        stores.append(copy)

    first_load.wait()
    for n in range(4):
        for copy in loads[n]:
            copy.wait()
        part = pl.ds(n * CHUNK, CHUNK)
        result[part, :] = (rows[part, :].astype(F32) + dot(mixed[part, :], wout[...])).astype(BF16)
        store(result.at[part], cand_out.at[n // 2, pl.ds(n % 2 * CHUNK, CHUNK)], n)
        if n == 0:
            hist_load.wait()
            store(hist_held, hist_out, 4)
    for copy in stores:
        copy.wait()


def body(
    tokens, item_table, w_in, w_out, gain_in, gain_attn, hist_len, row_start, impressions, item_slot
):
    vmem = pl.BlockSpec(memory_space=pltpu.VMEM)
    smem = pl.BlockSpec(memory_space=pltpu.SMEM)
    anywhere = pl.BlockSpec(memory_space=pl.ANY)
    half = jax.ShapeDtypeStruct((CANDS, WIDTH), BF16)
    hist, rows, mixed = pl.pallas_call(
        kernel,
        out_shape=(jax.ShapeDtypeStruct((ROWS, WIDTH), BF16), half, half),
        in_specs=[smem, smem, vmem, vmem, anywhere, anywhere, vmem, vmem, vmem, vmem],
        out_specs=(anywhere,) * 3,
        scratch_shapes=[
            pltpu.VMEM((4, WIDTH, WIDTH), BF16),
            pltpu.VMEM((WIDTH, WIDTH), BF16),
            pltpu.VMEM((4, ROWS, WIDTH), BF16),
            pltpu.VMEM((KEYS, WIDTH), BF16),
            pltpu.VMEM((KEYS, WIDTH), BF16),
            pltpu.VMEM((ROWS, WIDTH), BF16),
            pltpu.VMEM((ROWS, WIDTH), BF16),
            pltpu.VMEM((ROWS, WIDTH), F32),
            pltpu.VMEM((ROWS, KEYS), F32),
            pltpu.VMEM((ROWS, WIDTH), BF16),
            pltpu.VMEM((OWNERS, 1, 128), I32),
            pltpu.VMEM((NEAR * 8, 1, 128), I32),
            pltpu.VMEM((32, 1, 128), I32),
            pltpu.VMEM((ROWS, WIDTH), BF16),
            pltpu.VMEM((NEAR * CHUNK, WIDTH), BF16),
            pltpu.VMEM((4 * CHUNK, WIDTH), BF16),
            pltpu.VMEM((OWNERS * CAP, WIDTH), BF16),
            pltpu.VMEM((CANDS, WIDTH), F32),
            pltpu.VMEM((CANDS, WIDTH), BF16),
            pltpu.VMEM((CANDS, WIDTH), BF16),
            pltpu.VMEM((CANDS, WIDTH), BF16),
            pltpu.VMEM((CANDS, WIDTH), BF16),
            pltpu.VMEM((CANDS, WIDTH), F32),
            pltpu.VMEM((CANDS, WIDTH), BF16),
            pltpu.VMEM((CANDS, 128), I32),
            pltpu.SemaphoreType.DMA((5,)),
            pltpu.SemaphoreType.DMA,
            pltpu.SemaphoreType.DMA((NEAR,)),
            pltpu.SemaphoreType.DMA,
            pltpu.SemaphoreType.DMA,
            pltpu.SemaphoreType.DMA,
            pltpu.SemaphoreType.DMA((8,)),
            pltpu.SemaphoreType.DMA,
            pltpu.SemaphoreType.DMA((3,)),
            pltpu.SemaphoreType.DMA,
            pltpu.SemaphoreType.DMA,
            pltpu.SemaphoreType.DMA((2,)),
            pltpu.SemaphoreType.DMA((6,)),
        ],
        compiler_params=pltpu.CompilerParams(
            collective_id=0, has_side_effects=True, vmem_limit_bytes=56 * 2**20
        ),
    )(
        hist_len, row_start, tokens, item_table, w_in, w_out,
        gain_in.reshape(1, WIDTH), gain_attn.reshape(1, WIDTH),
        impressions, item_slot.reshape(128, 128),
    )
    return pl.pallas_call(
        output_kernel,
        out_shape=(
            jax.ShapeDtypeStruct((ROWS, WIDTH), BF16),
            jax.ShapeDtypeStruct((2, CANDS // 2, WIDTH), BF16),
        ),
        in_specs=[anywhere] * 4,
        out_specs=(anywhere, anywhere),
        scratch_shapes=[
            pltpu.VMEM((WIDTH, WIDTH), BF16),
            pltpu.VMEM((ROWS, WIDTH), BF16),
            pltpu.VMEM((CANDS, WIDTH), BF16),
            pltpu.VMEM((CANDS, WIDTH), BF16),
            pltpu.VMEM((CANDS, WIDTH), BF16),
            pltpu.SemaphoreType.DMA((10,)),
            pltpu.SemaphoreType.DMA((5,)),
        ],
        compiler_params=pltpu.CompilerParams(vmem_limit_bytes=56 * 2**20),
    )(hist, mixed, rows, w_out)


def solution(mesh):
    placed = (
        P(("users", "seq"), None),
        P("users", None),
        P(),
        P(),
        P(),
        P(),
        P("users"),
        P("users"),
        P("users", "seq"),
        P(),
    )
    return jax.shard_map(
        body,
        mesh=mesh,
        in_specs=placed,
        out_specs=(P(("users", "seq"), None), P("users", "seq", None)),
        check_vma=False,
    )
```

```python
import functools
import math

import jax
import jax.numpy as jnp
from jax import lax
from jax.experimental import pallas as pl
from jax.experimental.pallas import tpu as pltpu
from jax.sharding import PartitionSpec as P

MESH = pl.DeviceIdType.MESH
HEADS = 8
WIDTH = 1024
HEAD_DIM = WIDTH // HEADS
ROWS = 256
CANDS = 512
KEYS = 1024
CAP = 16
OWNERS = 64
NEAR = 5
CHUNK = 128
epsilon = 1e-05
F32 = jnp.float32
BF16 = jnp.bfloat16
I32 = jnp.int32


def group_dz(q):
    return [0, 1, 7, 2, 6, 3, 5, 4][q]


def group_of_dz(dz):
    return jnp.where(dz == 0, 0, jnp.where(dz <= 4, 2 * dz - 1, 2 * (8 - dz)))


def layer_norm(values, gain_row):
    centered = values - jnp.mean(values, axis=-1, keepdims=True)
    spread = jnp.mean(centered * centered, axis=-1, keepdims=True)
    return centered * lax.rsqrt(spread + epsilon) * gain_row


def half_silu(half):
    return half + half * jnp.tanh(half)


def dot(a, b):
    return jnp.dot(a, b, preferred_element_type=F32)


def dot_nt(a, b):
    return lax.dot_general(a, b, (((1,), (1,)), ((), ())), preferred_element_type=F32)


def dot_tn(a, b):
    return lax.dot_general(a, b, (((0,), (0,)), ((), ())), preferred_element_type=F32)


def iota(shape, dim):
    return lax.broadcasted_iota(I32, shape, dim)


def kernel(
    hist_len, row_start, tokens, table, w_in, w_out, gain_in, gain_attn, wanted, item_slot,
    hist_done, rows_done, mixed_done,
    win, wout, normed, keys, values, hgate, hquery, attended, scale_mask, hist,
    requests, asked, asked_far, far_table, served, served_far, embedded,
    rows_in, rows_out, cnormed, cgate, cquery, cattended, cmixed, place,
    w_sem, req_send, req_recv, far_req_recv, row_send, far_row_send, row_recv,
    ring_send, ring_recv, copy_up, copy_down, copy_recv, out_sem,
):
    me = lax.axis_index("users")
    y = lax.axis_index("seq")
    z, x, c = me // 8, (me // 2) % 4, me % 2
    half_scale = 0.5 / math.sqrt(HEAD_DIM)

    def device(zz, xx, cc, yy):
        return {"users": ((zz + 8) % 8) * 8 + ((xx + 4) % 4) * 2 + (cc + 2) % 2, "seq": (yy + 4) % 4}

    def remote(src, dst, send, recv, target):
        return pltpu.make_async_remote_copy(
            src_ref=src, dst_ref=dst, send_sem=send, recv_sem=recv, device_id=target, device_id_type=MESH
        )

    weight_copies = [
        pltpu.make_async_copy(w_in.at[:, pl.ds(b * WIDTH, WIDTH)], win.at[b], w_sem.at[b]) for b in range(4)
    ]
    weight_copies.append(pltpu.make_async_copy(w_out, wout, w_sem.at[4]))
    for copy in weight_copies:
        copy.start()

    barrier = pltpu.get_barrier_semaphore()
    def greet(target):
        pl.semaphore_signal(barrier, inc=1, device_id=target, device_id_type=MESH)

    for q in range(NEAR):
        for k in range(8):
            if q or k:
                greet(device(z + group_dz(q), x + k // 2, c + k % 2, y))
    for dy in (1, 2, 3):
        for k in range(8):
            greet(device(z, x + k // 2, c + k % 2, y + dy))
    greet(device(z + 3, x, c, y))
    greet(device(z + 5, x, c, y))

    pl.semaphore_wait(barrier, 65)

    phase = (z + 8 - y) % 4
    is_holder = phase != 2
    first_half, last_half = pl.ds(0, ROWS // 2), pl.ds(ROWS // 2, ROWS // 2)
    z_up, z_down = device(z + 1, x, c, y), device(z - 1, x, c, y)

    def copy_half(rows, send, index, plane):
        remote(
            table.at[rows], far_table.at[rows], send, copy_recv.at[index], device(plane, x, c, y)
        ).start()

    @pl.when(phase == 0)
    def _():
        copy_half(first_half, copy_up, 0, z + 3)
        copy_half(last_half, copy_down, 0, z - 3)

    ids = jnp.concatenate([wanted[0:1, :], wanted[1:2, :]], axis=1)
    pick_high = (iota((128, CANDS), 0) == (ids >> 7)).astype(BF16)
    slots_2d = item_slot[...]
    at_high = dot_tn((slots_2d >> 7).astype(F32).astype(BF16), pick_high) * 128.0 + dot_tn(
        (slots_2d & 127).astype(F32).astype(BF16), pick_high
    )
    slot = jnp.sum(jnp.where(iota((128, CANDS), 0) == (ids & 127), at_high, 0.0), axis=0, keepdims=True)
    slot = slot.astype(I32)
    owner, local = slot >> 8, slot & 255
    dz = ((owner >> 3) - z) & 7
    dx = (((owner >> 1) & 3) - x) & 3
    dc = (owner - c) & 1
    lot = group_of_dz(dz) * 8 + dx * 2 + dc
    is_lot = iota((OWNERS, CANDS), 0) == lot
    lot_hot = is_lot.astype(BF16)
    earlier = (iota((CANDS, CANDS), 0) < iota((CANDS, CANDS), 1)).astype(BF16)
    before = dot(lot_hot, earlier)
    rank = jnp.sum(jnp.where(is_lot, before, 0.0), axis=0, keepdims=True).astype(I32)
    lane = (lot & 7) * CAP + rank
    lane_local = jnp.where(iota((128, CANDS), 0) == lane, local, 0).astype(F32).astype(BF16)
    request_rows = dot_nt(lot_hot, lane_local).astype(I32)
    for j in range(OWNERS):
        requests[j] = request_rows[j : j + 1, :]
    asked[0] = request_rows[0:1, :]

    for q in range(8):
        dz = group_dz(q)
        if q < NEAR:
            for k in range(8):
                if q or k:
                    j = q * 8 + k
                    remote(
                        requests.at[j], asked.at[j], req_send, req_recv.at[q],
                        device(z + dz, x + k // 2, c + k % 2, y),
                    ).start()
        else:
            holder_y = (z + dz) % 4
            for k in range(8):
                j = q * 8 + k

                def ask(j=j, k=k, holder_y=holder_y, dz=dz):
                    remote(
                        requests.at[j], asked_far.at[y * 8 + k], req_send, far_req_recv,
                        device(z, x + k // 2, c + k % 2, holder_y),
                    ).start()

                if k:
                    ask()
                else:
                    pl.when(holder_y != y)(ask)

                    @pl.when(holder_y == y)
                    def _(j=j):
                        asked_far[y * 8] = requests[j]

    @pl.when(phase == 0)
    def _():
        copy_half(last_half, copy_up, 1, z + 3)
        copy_half(first_half, copy_down, 1, z - 3)

    up = device(z, x, c, y + 1)
    own = normed.at[y]
    normed[y] = layer_norm(tokens[...].astype(F32), gain_in[...]).astype(BF16)
    for dy in (1, 3, 2):
        remote(own, own, ring_send, ring_recv.at[dy - 1], device(z, x, c, y + dy)).start()

    place[:, 0:1] = jnp.sum(
        jnp.where(iota((CANDS, CANDS), 0) == iota((CANDS, CANDS), 1), lot * CAP + rank, 0).astype(F32),
        axis=1,
        keepdims=True,
    ).astype(I32)

    def gather(source, ask, first):
        gathered = ask[first]
        for k in range(1, 8):
            gathered = gathered + ask[first + k]
        pick = (iota((ROWS, CHUNK), 0) == gathered).astype(BF16)
        return dot_tn(pick, source[...]).astype(BF16)

    def send_near(q, k):
        rows = pl.ds(q * CHUNK + k * CAP, CAP)
        remote(
            served.at[rows], embedded.at[rows], row_send, row_recv.at[q],
            device(z - group_dz(q), x - k // 2, c - k % 2, y),
        ).start()

    for q in range(NEAR):
        first = 1 if q == 0 else 0
        lots = pl.ds(q * 8 + first, 8 - first)
        remote(asked.at[lots], asked.at[lots], req_send, req_recv.at[q], up).wait_recv()
        served[pl.ds(q * CHUNK, CHUNK), :] = gather(table, asked, q * 8)
        if q == 0:
            for k in range(1, 8):
                send_near(0, k)
            embedded[pl.ds(0, CAP), :] = served[pl.ds(0, CAP), :]

    @pl.when(phase == 3)
    def _():
        half = far_table.at[first_half]
        remote(half, half, copy_up, copy_recv.at[0], z_up).wait_recv()
        remote(half, half, copy_up, copy_recv.at[0], z_up).start()

    @pl.when(phase == 1)
    def _():
        half = far_table.at[last_half]
        remote(half, half, copy_down, copy_recv.at[0], z_down).wait_recv()
        remote(half, half, copy_down, copy_recv.at[1], z_down).start()

    def project(rows_value, block, write):
        def step(n, carry):
            columns = pl.ds(pl.multiple_of(n * 256, 256), 256)
            write(columns, dot(rows_value(), win[block, :, columns]))
            return carry

        lax.fori_loop(0, WIDTH // 256, step, 0, unroll=4)

    def project_keys(block):
        rows = pl.ds(pl.multiple_of(block * ROWS, ROWS), ROWS)

        def write_value(columns, out):
            values[rows, columns] = out.astype(BF16)

        def write_key(columns, out):
            keys[rows, columns] = out.astype(BF16)

        project(lambda: normed[block], 1, write_value)
        project(lambda: normed[block], 3, write_key)

    def write_hgate(columns, out):
        hgate[:, columns] = half_silu(out * 0.5).astype(BF16)

    def write_hquery(columns, out):
        hquery[:, columns] = out.astype(BF16)

    @pl.when(phase == 0)
    def _():
        half, other = far_table.at[first_half], far_table.at[last_half]
        remote(half, half, copy_up, copy_recv.at[0], z_up).wait_recv()
        remote(other, other, copy_up, copy_recv.at[1], z_up).wait_recv()

    @pl.when(phase % 2 == 1)
    def _():
        half = far_table.at[first_half]
        remote(half, half, copy_up, copy_recv.at[1], z_up).wait_recv()

    far_group = jnp.where(phase == 0, 7, jnp.where(phase == 3, 6, 5))
    far_base = pl.multiple_of(far_group * CHUNK, CHUNK)

    @pl.when(is_holder)
    def _():
        lots = asked_far.at[pl.ds(0, 31)]
        remote(lots, lots, req_send, far_req_recv, up).wait_recv()
        for dy in range(4):
            served_far[pl.ds(dy * CHUNK, CHUNK), :] = gather(far_table, asked_far, (y + dy) % 4 * 8)
        embedded[pl.ds(far_base, CAP), :] = served_far[0:CAP, :]

    for k in range(8):
        for q in range(1, NEAR):
            send_near(q, k)
            dy = q - 1
            if dy or k:

                @pl.when(is_holder)
                def _(dy=dy, k=k):
                    remote(
                        served_far.at[pl.ds(dy * CHUNK + k * CAP, CAP)],
                        embedded.at[pl.ds(pl.multiple_of(far_base + k * CAP, CAP), CAP)],
                        far_row_send, row_recv.at[far_group],
                        device(z, x - k // 2, c - k % 2, y + dy),
                    ).start()

    for copy in weight_copies:
        copy.wait()
    project(lambda: normed[y], 0, write_hgate)
    project(lambda: normed[y], 2, write_hquery)
    project_keys(y)

    for dy in (1, 3, 2):
        block = (y - dy + 4) % 4
        remote(normed.at[block], normed.at[block], ring_send, ring_recv.at[dy - 1], up).wait_recv()
        project_keys(block)

    def emit(source, target, index):
        copy = pltpu.make_async_copy(source, target, out_sem.at[index])
        copy.start()
        return copy

    emitted = []

    group_base = me * KEYS
    second = row_start[1] - group_base
    end_first, end_second = row_start[0] - group_base + hist_len[0], second + hist_len[1]

    def locate(spot):
        user = (spot >= second).astype(I32)
        return user, spot < jnp.where(user == 1, end_second, end_first)

    key_spot = iota((1, KEYS), 1)
    key_user, key_live = locate(key_spot)
    query_spot = y * ROWS + iota((ROWS, 1), 0)
    query_user, query_live = locate(query_spot)

    def attend(rows, query):
        def head(h, carry):
            columns = pl.ds(pl.multiple_of(h * HEAD_DIM, HEAD_DIM), HEAD_DIM)
            scores = dot_nt(query[:, columns], keys[:, columns])
            weights = half_silu(scores * scale_mask[0:rows, :]).astype(BF16)
            attended[0:rows, columns] = dot(weights, values[:, columns])
            return carry

        lax.fori_loop(0, HEADS, head, 0, unroll=4)

    def finish(rows, residual, gate, write):
        mixed = (layer_norm(attended[0:rows, :], gain_attn[...]) * gate[...].astype(F32)).astype(BF16)
        for n in range(WIDTH // 256):
            columns = pl.ds(n * 256, 256)
            write(columns, (residual(columns) + dot(mixed, wout[:, columns])).astype(BF16))

    allowed = (
        (query_user == key_user)
        & (query_live & key_live)
        & (key_spot <= query_spot)
    )
    scale_mask[...] = jnp.where(allowed, half_scale, 0.0)
    attend(ROWS, hquery)

    def write_hist(columns, out):
        hist[:, columns] = out

    finish(ROWS, lambda columns: tokens[:, columns].astype(F32), hgate, write_hist)

    emitted.append(emit(hist, hist_done, 0))

    def pick_rows(first, count):
        def part(n, carry):
            rows = pl.ds(pl.multiple_of(n * 256, 256), 256)
            pick = (iota((256, count), 1) + first == place[rows, 0:1]).astype(BF16)
            for m in range(WIDTH // 256):
                columns = pl.ds(m * 256, 256)
                found = dot(pick, embedded[pl.ds(first, count), columns])
                if first:
                    found = found + rows_in[rows, columns]
                rows_in[rows, columns] = found
            return carry

        lax.fori_loop(0, CANDS // 256, part, 0)

    for q in range(NEAR):
        rows = pl.ds(CAP, CHUNK - CAP) if q == 0 else pl.ds(q * CHUNK, CHUNK)
        remote(embedded.at[rows], embedded.at[rows], row_send, row_recv.at[q], up).wait_recv()
    pick_rows(0, NEAR * CHUNK)
    for q in range(NEAR, 8):
        own_copy = (z + group_dz(q)) % 4 == y

        @pl.when(own_copy)
        def _(q=q):
            rows = pl.ds(q * CHUNK + CAP, CHUNK - CAP)
            remote(embedded.at[rows], embedded.at[rows], row_send, row_recv.at[q], up).wait_recv()

        @pl.when(jnp.logical_not(own_copy))
        def _(q=q):
            rows = pl.ds(q * CHUNK, CHUNK)
            remote(embedded.at[rows], embedded.at[rows], row_send, row_recv.at[q], up).wait_recv()

    pick_rows(NEAR * CHUNK, (8 - NEAR) * CHUNK)

    def norm_rows(n, carry):
        rows = pl.ds(pl.multiple_of(n * CHUNK, CHUNK), CHUNK)
        value = rows_in[rows, :]
        rows_out[rows, :] = value.astype(BF16)
        cnormed[rows, :] = layer_norm(value, gain_in[...]).astype(BF16)
        return carry

    lax.fori_loop(0, CANDS // CHUNK, norm_rows, 0)
    emitted.append(emit(rows_out, rows_done, 1))

    def write_cquery(columns, out):
        cquery[:, columns] = out.astype(BF16)

    def write_cgate(columns, out):
        cgate[:, columns] = half_silu(out * 0.5).astype(BF16)

    project(lambda: cnormed[...], 2, write_cquery)

    lanes = iota((1, HEAD_DIM), 1)
    tile_lanes = iota((1, 256), 1)
    to_second = [(lanes * 0 + t * 256 >= second).astype(F32) for t in range(4)]
    to_first = [(lanes * 0 + t * 256 < second).astype(F32) for t in range(4)]
    shared = second >> 8
    is_shared = [(lanes * 0 + t == shared).astype(F32).astype(BF16) for t in range(4)]

    def tile_scale(spot, second_rows):
        low = jnp.where(second_rows, second, 0)
        high = jnp.where(second_rows, end_second, end_first)
        return jnp.where((spot >= low) & (spot < high), half_scale, 0.0)

    scales = [tile_scale(tile_lanes + t * 256, tile_lanes * 0 + t * 256 >= second) for t in range(4)]
    shared_spot = tile_lanes + shared * 256
    shared_live = (shared_spot >= second) & (shared_spot < end_second) & (tile_lanes * 0 + shared * 256 < second)
    shared_scale = jnp.where(shared_live, half_scale, 0.0)

    def cand_head(h, carry):
        columns = pl.ds(pl.multiple_of(h * HEAD_DIM, HEAD_DIM), HEAD_DIM)
        first_query, second_query = cquery[0:256, columns], cquery[256:512, columns]

        def weigh(query, key, value, scale):
            return dot(half_silu(dot_nt(query, key) * scale).astype(BF16), value)

        key_shared = value_shared = None
        for t in range(4):
            span = pl.ds(t * 256, 256)
            key, value = keys[span, columns], values[span, columns]
            if t == 0:
                key_shared, value_shared = key * is_shared[t], value * is_shared[t]
                cattended[0:256, columns] = weigh(first_query, key, value, scales[t])
                continue
            key_shared = key_shared + key * is_shared[t]
            value_shared = value_shared + value * is_shared[t]
            query = first_query * to_first[t].astype(BF16) + second_query * to_second[t].astype(BF16)
            found = weigh(query, key, value, scales[t])
            cattended[0:256, columns] += found * to_first[t]
            if t == 1:
                cattended[256:512, columns] = found * to_second[t]
            else:
                cattended[256:512, columns] += found * to_second[t]
        cattended[256:512, columns] += weigh(second_query, key_shared, value_shared, shared_scale)
        return carry

    lax.fori_loop(0, HEADS, cand_head, 0, unroll=4)
    project(lambda: cnormed[...], 0, write_cgate)
    for n in range(4):
        rows = pl.ds(n * CHUNK, CHUNK)
        mixed = layer_norm(cattended[rows, :], gain_attn[...]) * cgate[rows, :].astype(F32)
        cmixed[rows, :] = mixed.astype(BF16)
        emitted.append(emit(cmixed.at[rows], mixed_done.at[rows], 2 + n))

    others = normed.at[pl.ds(0, 3)]
    remote(others, others, ring_send, ring_recv.at[0], up).wait_send()
    lots = requests.at[pl.ds(0, OWNERS - 2)]
    remote(lots, lots, req_send, req_recv.at[0], up).wait_send()

    @pl.when(jnp.logical_not(is_holder))
    def _():
        remote(requests.at[0], requests.at[0], req_send, req_recv.at[0], up).wait_send()

    rows = served.at[pl.ds(CAP, NEAR * CHUNK - CAP)]
    remote(rows, rows, row_send, row_recv.at[0], up).wait_send()

    @pl.when(is_holder)
    def _():
        rows = served_far.at[pl.ds(CAP, 4 * CHUNK - CAP)]
        remote(rows, rows, far_row_send, row_recv.at[0], up).wait_send()

    @pl.when(phase == 0)
    def _():
        remote(far_table, far_table, copy_up, copy_recv.at[0], z_up).wait_send()
        remote(far_table, far_table, copy_down, copy_recv.at[0], z_down).wait_send()

    @pl.when(phase == 3)
    def _():
        half = far_table.at[first_half]
        remote(half, half, copy_up, copy_recv.at[0], z_up).wait_send()

    @pl.when(phase == 1)
    def _():
        half = far_table.at[last_half]
        remote(half, half, copy_down, copy_recv.at[0], z_down).wait_send()

    for copy in emitted:
        copy.wait()


def output_kernel(
    hist, mixed_in, rows_in, w_out, hist_out, cand_out, wout, hist_held, mixed, rows, result, sem, out_sem
):
    def load(source, target, index):
        copy = pltpu.make_async_copy(source, target, sem.at[index])
        copy.start()
        return copy

    first_load = load(w_out, wout, 9)
    loads = []
    for n in range(4):
        part = pl.ds(n * CHUNK, CHUNK)
        loads.append(
            (load(mixed_in.at[part], mixed.at[part], 2 * n), load(rows_in.at[part], rows.at[part], 2 * n + 1))
        )
    hist_load = load(hist, hist_held, 8)
    stores = []

    def store(source, target, index):
        copy = pltpu.make_async_copy(source, target, out_sem.at[index])
        copy.start()
        stores.append(copy)

    first_load.wait()
    for n in range(4):
        for copy in loads[n]:
            copy.wait()
        part = pl.ds(n * CHUNK, CHUNK)
        result[part, :] = (rows[part, :].astype(F32) + dot(mixed[part, :], wout[...])).astype(BF16)
        store(result.at[part], cand_out.at[n // 2, pl.ds(n % 2 * CHUNK, CHUNK)], n)
        if n == 0:
            hist_load.wait()
            store(hist_held, hist_out, 4)
    for copy in stores:
        copy.wait()


def body(
    tokens, item_table, w_in, w_out, gain_in, gain_attn, hist_len, row_start, impressions, item_slot
):
    vmem = pl.BlockSpec(memory_space=pltpu.VMEM)
    smem = pl.BlockSpec(memory_space=pltpu.SMEM)
    anywhere = pl.BlockSpec(memory_space=pl.ANY)
    half = jax.ShapeDtypeStruct((CANDS, WIDTH), BF16)
    hist, rows, mixed = pl.pallas_call(
        kernel,
        out_shape=(jax.ShapeDtypeStruct((ROWS, WIDTH), BF16), half, half),
        in_specs=[smem, smem, vmem, vmem, anywhere, anywhere, vmem, vmem, vmem, vmem],
        out_specs=(anywhere,) * 3,
        scratch_shapes=[
            pltpu.VMEM((4, WIDTH, WIDTH), BF16),
            pltpu.VMEM((WIDTH, WIDTH), BF16),
            pltpu.VMEM((4, ROWS, WIDTH), BF16),
            pltpu.VMEM((KEYS, WIDTH), BF16),
            pltpu.VMEM((KEYS, WIDTH), BF16),
            pltpu.VMEM((ROWS, WIDTH), BF16),
            pltpu.VMEM((ROWS, WIDTH), BF16),
            pltpu.VMEM((ROWS, WIDTH), F32),
            pltpu.VMEM((ROWS, KEYS), F32),
            pltpu.VMEM((ROWS, WIDTH), BF16),
            pltpu.VMEM((OWNERS, 1, 128), I32),
            pltpu.VMEM((NEAR * 8, 1, 128), I32),
            pltpu.VMEM((32, 1, 128), I32),
            pltpu.VMEM((ROWS, WIDTH), BF16),
            pltpu.VMEM((NEAR * CHUNK, WIDTH), BF16),
            pltpu.VMEM((4 * CHUNK, WIDTH), BF16),
            pltpu.VMEM((OWNERS * CAP, WIDTH), BF16),
            pltpu.VMEM((CANDS, WIDTH), F32),
            pltpu.VMEM((CANDS, WIDTH), BF16),
            pltpu.VMEM((CANDS, WIDTH), BF16),
            pltpu.VMEM((CANDS, WIDTH), BF16),
            pltpu.VMEM((CANDS, WIDTH), BF16),
            pltpu.VMEM((CANDS, WIDTH), F32),
            pltpu.VMEM((CANDS, WIDTH), BF16),
            pltpu.VMEM((CANDS, 128), I32),
            pltpu.SemaphoreType.DMA((5,)),
            pltpu.SemaphoreType.DMA,
            pltpu.SemaphoreType.DMA((NEAR,)),
            pltpu.SemaphoreType.DMA,
            pltpu.SemaphoreType.DMA,
            pltpu.SemaphoreType.DMA,
            pltpu.SemaphoreType.DMA((8,)),
            pltpu.SemaphoreType.DMA,
            pltpu.SemaphoreType.DMA((3,)),
            pltpu.SemaphoreType.DMA,
            pltpu.SemaphoreType.DMA,
            pltpu.SemaphoreType.DMA((2,)),
            pltpu.SemaphoreType.DMA((6,)),
        ],
        compiler_params=pltpu.CompilerParams(
            collective_id=0, has_side_effects=True, vmem_limit_bytes=56 * 2**20
        ),
    )(
        hist_len, row_start, tokens, item_table, w_in, w_out,
        gain_in.reshape(1, WIDTH), gain_attn.reshape(1, WIDTH),
        impressions, item_slot.reshape(128, 128),
    )
    return pl.pallas_call(
        output_kernel,
        out_shape=(
            jax.ShapeDtypeStruct((ROWS, WIDTH), BF16),
            jax.ShapeDtypeStruct((2, CANDS // 2, WIDTH), BF16),
        ),
        in_specs=[anywhere] * 4,
        out_specs=(anywhere, anywhere),
        scratch_shapes=[
            pltpu.VMEM((WIDTH, WIDTH), BF16),
            pltpu.VMEM((ROWS, WIDTH), BF16),
            pltpu.VMEM((CANDS, WIDTH), BF16),
            pltpu.VMEM((CANDS, WIDTH), BF16),
            pltpu.VMEM((CANDS, WIDTH), BF16),
            pltpu.SemaphoreType.DMA((10,)),
            pltpu.SemaphoreType.DMA((5,)),
        ],
        compiler_params=pltpu.CompilerParams(vmem_limit_bytes=56 * 2**20),
    )(hist, mixed, rows, w_out)


def solution(mesh):
    placed = (
        P(("users", "seq"), None),
        P("users", None),
        P(),
        P(),
        P(),
        P(),
        P("users"),
        P("users"),
        P("users", "seq"),
        P(),
    )
    return jax.shard_map(
        body,
        mesh=mesh,
        in_specs=placed,
        out_specs=(P(("users", "seq"), None), P("users", "seq", None)),
        check_vma=False,
    )
```
